32 devices in a mesh: groups: 2 (over x), shard: 16 (over z, y, core).
Axes of the slice: x: 2, y: 2, z: 4, core: 2. Of those that a mesh axis runs over, the one named last changes fastest.
Arguments:
- item_table: bfloat16 [65536, 128], P('shard'), may hold values from -3 to 3
- row_accum: float32 [65536], P('shard'), may hold values from 0.1 to 1
- serving_table: bfloat16 [65536, 128], P('shard'), may hold values from -3 to 3
- grad_rows: bfloat16 [512, 128, 128], P(('groups', 'shard')), parts along dimension 0, may hold values from -6 to 6
- grad_ids: int32 [512, 128], P(('groups', 'shard')), parts along dimension 0, may hold values from 0 to 4095
- grad_counts: int32 [512], P(('groups', 'shard')), parts along dimension 0, may hold values from 1 to 128, as said below
- request_ids: int32 [512, 480], P(('groups', 'shard')), parts along dimension 0, may hold values from 0 to 4095
- request_slots: int32 [32768, 5], P(('groups', 'shard')), parts along dimension 0, may hold values from 0 to 7679, as said below
- cross_weight: bfloat16 [3, 640, 640], replicated, may hold values from -0.25 to 0.25
- cross_bias: bfloat16 [3, 640], replicated, may hold values from -3 to 3
- tower_weight: bfloat16 [640, 4096], replicated, may hold values from -0.25 to 0.25
- tower_bias: bfloat16 [4096], replicated, may hold values from -3 to 3
- score_weight: bfloat16 [4096], replicated, may hold values from -0.09375 to 0.09375
Outputs:
- new_table: bfloat16 [131072, 128], P(('groups', 'shard')), parts along dimension 0
- new_accum: float32 [131072], P(('groups', 'shard')), parts along dimension 0
- new_serving: bfloat16 [131072, 128], P(('groups', 'shard')), parts along dimension 0
- scores: float32 [32768], P(('groups', 'shard')), parts along dimension 0
The draws below stay inside these ranges and needn't reach their ends.
There are 2 independent parts, one for each index of `groups`. The reference program is written for one: setup_inputs(seed, part) draws one part's arguments, and reference() takes and returns one part's arrays. A program takes and returns all parts, laid end to end along the dimension named above; an argument that names none is the same for every part. Nothing has to cross between parts.
Inputs may be any that keep to these rules, and one draw needn't show every extreme that they name: `grad_counts`: one owner, drawn from the seed, has all 128 slots used in the block of every device; slots past a count are padding. `grad_ids`: rows within the owner's block; slots past a count may hold any row. `request_ids`: slots that no request reads may hold any row. `request_slots`: all slots named by the requests of one device are distinct; every device uses all 480 slots of some owner.
All inputs are finite; a program needn't handle non-finite values. Where the reference program divides by a largest or mean magnitude, that divisor is 1e-20 or more.
Results may differ from the reference program's by a relative error of at most 0.012.
Values may be sent and summed in bfloat16 or wider, within the bound.
No kernel may reach another device: no remote copies, remote signals or barrier semaphores. Data moves between devices by JAX's collectives and lax.ppermute only.
A program may use at most 64 MiB of HBM per device.

```python
import math
import jax
import jax.numpy as jnp
from jax import lax

E = 128
FF = 4096
ROWS_DEV = 4096
REQ_DEV = 1024
FEAT = 5
CROSS = 3
X = 640
CAP = 128
CAPR = 480
ROWS = 65536
REQ_TOTAL = 16384
N_SHARD = 16


def draw_grad_counts(key, part):
    key = jax.random.fold_in(key, 11)
    key_hot, key_level, key_count = jax.random.split(key, 3)
    hot_owner = jax.random.randint(key_hot, (), 0, N_SHARD)
    owners = jnp.arange(N_SHARD)
    levels = jax.random.randint(key_level, (N_SHARD,), 1, CAP + 1)
    levels = jnp.where(owners == hot_owner, CAP, levels)
    counts = jax.random.randint(key_count, (N_SHARD, N_SHARD), 1, levels[None, :] + 1)
    counts = jnp.where(owners[None, :] == hot_owner, CAP, counts)
    return counts.reshape(-1).astype(jnp.int32)


def draw_request_slots(key, part):
    key = jax.random.fold_in(key, 23)
    slot_total = N_SHARD * CAPR

    def draw_device(device_key):
        key_level, key_first, key_jitter, key_order = jax.random.split(device_key, 4)
        levels = jax.random.randint(key_level, (N_SHARD,), 0, 4)
        first_owner = jax.random.randint(key_first, (), 0, N_SHARD)
        levels = jnp.where(jnp.arange(N_SHARD) == first_owner, 0, levels)
        owner_of = jnp.arange(slot_total) // CAPR
        jitter = jax.random.randint(key_jitter, (slot_total,), 0, 1024)
        scored = (levels[owner_of] * 1024 + jitter) * slot_total + jnp.arange(slot_total)
        chosen = jnp.argsort(scored)[:REQ_DEV * FEAT]
        chosen = jax.random.permutation(key_order, chosen)
        return chosen.reshape(REQ_DEV, FEAT)
    device_keys = jax.random.split(key, N_SHARD)
    return jax.vmap(draw_device)(device_keys).reshape(N_SHARD * REQ_DEV, FEAT).astype(jnp.int32)


def with_ends(values, own_key, least, largest):
    extent = values.shape
    place = [jax.random.randint(jax.random.fold_in(own_key, axis), (), 0, extent[axis]) for axis in range(len(extent))]
    values = values.at[tuple(place)].set(least)
    longest = extent.index(max(extent))
    place[longest] = (place[longest] + 1) % extent[longest]
    return values.at[tuple(place)].set(largest)


def block_levels(own_key, extent, pieces, least, high):
    factor_of, own = 1.0, jax.random.fold_in(own_key, 6)
    for dim, blocks in pieces:
        heights = jnp.exp(jax.random.uniform(jax.random.fold_in(own, dim), (blocks,), jnp.float32, least / len(pieces), high / len(pieces)))
        factor_of = factor_of * jnp.repeat(heights, extent[dim] // blocks).reshape([-1 if axis == dim else 1 for axis in range(len(extent))])
    return factor_of


def scatter_about(key, dims, deviation, most, cuts=(), held_as=jnp.bfloat16):
    loudness = block_levels(key, dims, cuts, -0.22, 0.18) if cuts else 1.0
    entries = jax.random.normal(key, dims, jnp.float32) * deviation * loudness
    return jnp.minimum(jnp.maximum(entries, -most), most).astype(held_as)


def setup_inputs(seed: int = 0, part: int = 0) -> dict:
    keys = jax.random.split(jax.random.key(seed), 14)
    part_splits = jax.random.split(jax.random.fold_in(keys[13], part), 14)
    item_table = scatter_about(keys[0], (ROWS, E), 0.5, 3.0, ((0, 16),))
    row_accum = jnp.clip(jnp.exp(math.log(1.0) - 2.3025851 * jax.random.uniform(keys[1], (ROWS,), jnp.float32) ** block_levels(keys[1], (ROWS,), ((0, 16),), -0.2, 0.2)), 0.1, 1.0)
    serving_table = scatter_about(keys[2], (ROWS, E), 0.5, 3.0, ((0, 16),))
    grad_rows = scatter_about(part_splits[3], (N_SHARD * N_SHARD, CAP, E), 1.0, 6.0, ((0, 16),))
    grad_ids = with_ends(jax.random.randint(part_splits[4], (N_SHARD * N_SHARD, CAP), 0, ROWS_DEV), jax.random.fold_in(part_splits[4], 1), 0, ROWS_DEV - 1).astype(jnp.int32)
    grad_counts = draw_grad_counts(jax.random.fold_in(jax.random.fold_in(keys[13], part), 71), part)
    request_ids = with_ends(jax.random.randint(part_splits[6], (N_SHARD * N_SHARD, CAPR), 0, ROWS_DEV), jax.random.fold_in(part_splits[6], 1), 0, ROWS_DEV - 1).astype(jnp.int32)
    request_slots = draw_request_slots(jax.random.fold_in(jax.random.fold_in(keys[13], part), 71), part)
    cross_weight = scatter_about(keys[8], (CROSS, X, X), X ** -0.5, 0.25)
    cross_bias = scatter_about(keys[9], (CROSS, X), 0.5, 3.0)
    tower_weight = scatter_about(keys[10], (X, FF), X ** -0.5, 0.25)
    tower_bias = scatter_about(keys[11], (FF,), 0.5, 3.0)
    score_weight = scatter_about(keys[12], (FF,), FF ** -0.5, 0.09375)
    return dict(item_table=item_table, row_accum=row_accum, serving_table=serving_table, grad_rows=grad_rows, grad_ids=grad_ids, grad_counts=grad_counts, request_ids=request_ids, request_slots=request_slots, cross_weight=cross_weight, cross_bias=cross_bias, tower_weight=tower_weight, tower_bias=tower_bias, score_weight=score_weight)


LEARN_RATE = 0.5
SCALE_FLOOR = 0.25

def tower_scores(request_block, cross_weight, cross_bias, tower_weight, tower_bias, score_weight):
    crossed = request_block
    base_values = request_block.astype(jnp.float32)
    for layer_index in range(CROSS):
        projected = jnp.dot(crossed, cross_weight[layer_index], preferred_element_type=jnp.float32)
        projected = projected + cross_bias[layer_index].astype(jnp.float32)
        crossed = (base_values * projected + crossed.astype(jnp.float32)).astype(jnp.bfloat16)
    hidden = jnp.dot(crossed, tower_weight, preferred_element_type=jnp.float32) + tower_bias.astype(jnp.float32)
    hidden = jnp.maximum(hidden, 0.0).astype(jnp.bfloat16)
    return jnp.dot(hidden, score_weight, preferred_element_type=jnp.float32)

def reference(item_table, row_accum, serving_table, grad_rows, grad_ids, grad_counts, request_ids, request_slots, cross_weight, cross_bias, tower_weight, tower_bias, score_weight):
    blocks = N_SHARD * N_SHARD
    slot_index = jnp.arange(CAP, dtype=jnp.int32)
    is_valid = slot_index[None, :] < grad_counts[:, None]
    owners = jnp.arange(blocks, dtype=jnp.int32) % N_SHARD
    target = (owners[:, None] * ROWS_DEV + grad_ids).reshape(-1).astype(jnp.int32)
    values = jnp.where(is_valid[:, :, None], grad_rows.astype(jnp.float32), 0.0).reshape(-1, E)
    grad_sum = jnp.zeros((ROWS, E), jnp.float32).at[target].add(values)
    new_accum = row_accum + lax.optimization_barrier(jnp.mean(grad_sum * grad_sum, axis=1))
    step_rows = LEARN_RATE * grad_sum / jnp.sqrt(new_accum)[:, None]
    new_table = (item_table.astype(jnp.float32) - step_rows).astype(jnp.bfloat16)
    row_delta = new_table.astype(jnp.float32) - item_table.astype(jnp.float32)
    grouped = row_delta.reshape(ROWS, E // 32, 32)
    scales = jnp.maximum(lax.optimization_barrier(jnp.max(jnp.abs(grouped), axis=2)), SCALE_FLOOR).astype(jnp.bfloat16)
    payload = (grouped / scales.astype(jnp.float32)[:, :, None]).astype(jnp.bfloat16)
    decoded = (payload.astype(jnp.float32) * scales.astype(jnp.float32)[:, :, None]).reshape(ROWS, E)
    new_serving = (serving_table.astype(jnp.float32) + jnp.roll(decoded, ROWS_DEV, axis=0)).astype(jnp.bfloat16)
    serve_block = (owners + 1) % N_SHARD
    where_rows = (serve_block[:, None] * ROWS_DEV + request_ids).reshape(-1).astype(jnp.int32)
    device = jnp.arange(REQ_TOTAL, dtype=jnp.int32) // REQ_DEV
    flat_index = (device[:, None] * (N_SHARD * CAPR) + request_slots).reshape(-1).astype(jnp.int32)
    features = new_serving[where_rows[flat_index]].reshape(N_SHARD, REQ_DEV, X)

    def score_block(request_block):
        return tower_scores(request_block, cross_weight, cross_bias, tower_weight, tower_bias, score_weight)
    scores = lax.map(score_block, features).reshape(REQ_TOTAL)
    return (new_table, new_accum, new_serving, scores)
```

```python
import functools
import jax
import jax.numpy as jnp
from jax import lax
from jax.experimental import pallas as pl
from jax.experimental.pallas import tpu as pltpu
from jax.sharding import PartitionSpec as P

LEARN_RATE = 0.5
SCALE_FLOOR = 0.25
LANES = 128
DIGIT = 64
TILE = 256
MIB = 1024 * 1024


def ceil_to(value, unit):
    return -(-value // unit) * unit


def pack_kernel(cap, meta_rows, req_rows, rows_ref, ids_ref, counts_ref, req_ref, out_ref, meta_ref):
    blocks = rows_ref.shape[0]
    f32 = jnp.float32
    out_ref[:, :cap, :] = rows_ref[...]
    meta_ref[...] = jnp.zeros_like(meta_ref)
    slot = lax.broadcasted_iota(jnp.int32, ids_ref.shape, 1)
    ids = ids_ref[...]
    valid = slot < counts_ref[...]
    high = jnp.where(valid, ids // TILE, TILE - 1).astype(f32)
    low = (ids % TILE).astype(f32)
    width = ids.shape[1]
    meta_ref[:, 0, :width] = high
    meta_ref[:, 1, :width] = low
    for row in range(req_rows):
        start = row * LANES
        stop = min(start + LANES, req_ref.shape[1])
        part = req_ref[:, start:stop]
        meta_ref[:, 2 + row, : stop - start] = (part // DIGIT).astype(f32)
        meta_ref[:, 2 + req_rows + row, : stop - start] = (part % DIGIT).astype(f32)
    out_ref[:, cap:, :] = meta_ref[...].astype(jnp.bfloat16)


def update_kernel(
    cap, req_at, req_rows, recv_ref, req_ref, accum_ref, item_ref, serving_ref,
    table_out, accum_out, serving_out, live_out, req_out,
):
    f32, bf16 = jnp.float32, jnp.bfloat16
    blocks = recv_ref.shape[0]
    row_count = item_ref.shape[0]
    req_high = req_ref[:, req_at : req_at + req_rows, :].astype(f32)
    req_low = req_ref[:, req_at + req_rows : req_at + 2 * req_rows, :].astype(f32)
    req_out[...] = (req_high * DIGIT + req_low).astype(jnp.int32)
    values = recv_ref[:, :cap, :].reshape(blocks * cap, LANES)
    row_in_tile = lax.broadcasted_iota(jnp.int32, (TILE, LANES), 0).astype(f32)
    lane = lax.broadcasted_iota(jnp.int32, (TILE, LANES), 1)
    eye = lax.broadcasted_iota(jnp.int32, (LANES, LANES), 0) == lax.broadcasted_iota(
        jnp.int32, (LANES, LANES), 1
    )
    source = lax.broadcasted_iota(jnp.int32, (LANES, LANES), 0)
    target = lax.broadcasted_iota(jnp.int32, (LANES, LANES), 1)
    spread = jnp.where(source == (target // 32) * 32 + 31, 1.0, 0.0).astype(bf16)
    high = [recv_ref[b, cap : cap + 1, :].astype(f32) for b in range(blocks)]
    low = [recv_ref[b, cap + 1 : cap + 2, :].astype(f32) for b in range(blocks)]

    def step(t, carry):
        here = t.astype(f32)
        marks = [
            jnp.where(row_in_tile == jnp.where(high[b] == here, low[b], -1.0), 1.0, 0.0).astype(bf16)
            for b in range(blocks)
        ]
        grad = jnp.dot(jnp.concatenate(marks, axis=1), values, preferred_element_type=f32)
        rows = pl.ds(pl.multiple_of(t * TILE, TILE), TILE)
        mean = jnp.sum(grad * grad, axis=1, keepdims=True) * (1.0 / LANES)
        columns = []
        for half in range(TILE // LANES):
            line = accum_ref[pl.ds(t * (TILE // LANES) + half, 1), :]
            column = jnp.sum(jnp.where(eye, line, 0.0), axis=1, keepdims=True)
            column = column + mean[half * LANES : (half + 1) * LANES]
            accum_out[pl.ds(t * (TILE // LANES) + half, 1), :] = jnp.sum(
                jnp.where(eye, column, 0.0), axis=0, keepdims=True
            )
            columns.append(column)
        accum = jnp.concatenate(columns, axis=0)
        item = item_ref[rows, :].astype(f32)
        fresh = (item - LEARN_RATE * grad / jnp.sqrt(accum)).astype(bf16)
        table_out[rows, :] = fresh
        delta = fresh.astype(f32) - item
        top = jnp.abs(delta)
        for shift in (1, 2, 4, 8, 16):
            top = jnp.maximum(top, pltpu.roll(top, shift, 1))
        scale = jnp.where(lane % 32 == 31, jnp.maximum(top, SCALE_FLOOR), 0.0).astype(bf16)
        scale = jnp.dot(scale, spread, preferred_element_type=f32)
        payload = (delta / scale).astype(bf16)
        serving = (serving_ref[rows, :].astype(f32) + payload.astype(f32) * scale).astype(bf16)
        serving_out[rows, :] = serving
        live_out[rows, :] = serving.astype(f32)
        return carry

    lax.fori_loop(0, row_count // TILE, step, 0)


def gather_kernel(width, pitch, ids_ref, live_ref, out_ref, line_ref):
    blocks = out_ref.shape[0]
    unroll = 8

    def block(b, carry):
        def rows(k, inner):
            for u in range(unroll):
                j = k * unroll + u
                line_ref[pl.ds(j, 1), :] = live_ref[pl.ds(ids_ref[b * pitch + j], 1), :]
            return inner

        lax.fori_loop(0, width // unroll, rows, 0)
        out_ref[b] = line_ref[...].astype(jnp.bfloat16)
        return carry

    lax.fori_loop(0, blocks, block, 0)


def tower_kernel(
    slots_ref, fetched_ref, cross_ref, cross_bias_ref, tower_ref, tower_bias_ref, score_ref,
    out_ref, wide_ref, base_ref, crossed_ref, sum_ref,
):
    f32, bf16 = jnp.float32, jnp.bfloat16
    feats, requests, _ = base_ref.shape
    hidden = tower_ref.shape[1]
    wide_ref[...] = fetched_ref[...].astype(f32)
    unroll = 8

    def collect(k, carry):
        for f in range(feats):
            for u in range(unroll):
                r = k * unroll + u
                base_ref[f, pl.ds(r, 1), :] = wide_ref[pl.ds(slots_ref[f, r], 1), :]
        return carry

    lax.fori_loop(0, requests // unroll, collect, 0)
    for f in range(feats):
        crossed_ref[:, f * LANES : (f + 1) * LANES] = base_ref[f].astype(bf16)
    chunk = 256
    for layer in range(cross_ref.shape[0]):
        def cross(k, carry):
            rows = pl.ds(pl.multiple_of(k * chunk, chunk), chunk)
            old = crossed_ref[rows, :]
            projected = jnp.dot(old, cross_ref[layer], preferred_element_type=f32)
            projected = projected + cross_bias_ref[layer : layer + 1, :].astype(f32)
            base = jnp.concatenate([base_ref[f, rows, :] for f in range(feats)], axis=1)
            crossed_ref[rows, :] = (base * projected + old.astype(f32)).astype(bf16)
            return carry

        lax.fori_loop(0, requests // chunk, cross, 0)
    sum_ref[...] = jnp.zeros_like(sum_ref)

    def tower(k, carry):
        cols = pl.ds(pl.multiple_of(k * chunk, chunk), chunk)
        raw = jnp.dot(crossed_ref[...], tower_ref[:, cols], preferred_element_type=f32)
        raw = jnp.maximum(raw + tower_bias_ref[:, cols].astype(f32), 0.0)
        raw = raw * score_ref[:, cols].astype(f32)
        sum_ref[...] += raw[:, :LANES] + raw[:, LANES:]
        return carry

    lax.fori_loop(0, hidden // chunk, tower, 0)
    eye = lax.broadcasted_iota(jnp.int32, (LANES, LANES), 0) == lax.broadcasted_iota(
        jnp.int32, (LANES, LANES), 1
    )
    for k in range(requests // LANES):
        column = jnp.sum(sum_ref[k * LANES : (k + 1) * LANES, :], axis=1, keepdims=True)
        out_ref[k : k + 1, :] = jnp.sum(jnp.where(eye, column, 0.0), axis=0, keepdims=True)


def body(
    item_table, row_accum, serving_table, grad_rows, grad_ids, grad_counts, request_ids,
    request_slots, cross_weight, cross_bias, tower_weight, tower_bias, score_weight,
):
    f32, bf16 = jnp.float32, jnp.bfloat16
    shards = lax.axis_size("shard")
    row_count, emb = item_table.shape
    cap, capr = grad_ids.shape[1], request_ids.shape[1]
    requests, feats = request_slots.shape
    req_rows = ceil_to(capr, LANES) // LANES
    meta_rows = ceil_to(2 + 2 * req_rows, 16)
    vmem = pl.BlockSpec(memory_space=pltpu.VMEM)
    smem = pl.BlockSpec(memory_space=pltpu.SMEM)
    params = functools.partial(pltpu.CompilerParams, vmem_limit_bytes=40 * MIB)

    behind = [(i, (i - 1) % shards) for i in range(shards)]
    ahead = [(i, (i + 1) % shards) for i in range(shards)]
    serving_here = lax.ppermute(serving_table, "shard", behind)

    packed = pl.pallas_call(
        functools.partial(pack_kernel, cap, meta_rows, req_rows),
        out_shape=jax.ShapeDtypeStruct((shards, cap + meta_rows, emb), bf16),
        in_specs=[vmem] * 4,
        out_specs=vmem,
        scratch_shapes=[pltpu.VMEM((shards, meta_rows, LANES), f32)],
        compiler_params=params(),
        name="pack",
    )(grad_rows, grad_ids, grad_counts.reshape(shards, 1), request_ids)
    recv = lax.all_to_all(packed, "shard", split_axis=0, concat_axis=0, tiled=True)

    joined = recv
    if cap < LANES:
        groups = shards * cap // LANES
        marks = recv[:, cap : cap + 2, :cap].reshape(groups, LANES // cap, 2, cap)
        marks = marks.transpose(0, 2, 1, 3).reshape(groups, 2, LANES)
        marks = jnp.pad(marks, ((0, 0), (0, 14), (0, 0)))
        joined = jnp.concatenate([recv[:, :cap, :].reshape(groups, LANES, emb), marks], axis=1)

    new_table, new_accum, serving_next, live, req = pl.pallas_call(
        functools.partial(update_kernel, LANES, cap + 2, req_rows),
        out_shape=(
            jax.ShapeDtypeStruct((row_count, emb), bf16),
            jax.ShapeDtypeStruct((row_count // LANES, LANES), f32),
            jax.ShapeDtypeStruct((row_count, emb), bf16),
            jax.ShapeDtypeStruct((row_count, emb), f32),
            jax.ShapeDtypeStruct((shards, req_rows, LANES), jnp.int32),
        ),
        in_specs=[vmem] * 5,
        out_specs=(vmem,) * 5,
        compiler_params=params(),
        name="update",
    )(joined, recv, row_accum.reshape(-1, LANES), item_table, serving_here)

    found = pl.pallas_call(
        functools.partial(gather_kernel, capr, req_rows * LANES),
        out_shape=jax.ShapeDtypeStruct((shards, capr, emb), bf16),
        in_specs=[smem, vmem],
        out_specs=vmem,
        scratch_shapes=[pltpu.VMEM((capr, emb), f32)],
        compiler_params=params(),
        name="gather",
    )(req.reshape(-1), live)
    fetched = lax.all_to_all(found, "shard", split_axis=0, concat_axis=0, tiled=True)
    new_serving = lax.ppermute(serving_next, "shard", ahead)

    scores = pl.pallas_call(
        tower_kernel,
        out_shape=jax.ShapeDtypeStruct((requests // LANES, LANES), f32),
        in_specs=[smem] + [vmem] * 6,
        out_specs=vmem,
        scratch_shapes=[
            pltpu.VMEM((shards * capr, emb), f32),
            pltpu.VMEM((feats, requests, emb), f32),
            pltpu.VMEM((requests, feats * emb), bf16),
            pltpu.VMEM((requests, LANES), f32),
        ],
        compiler_params=params(),
        name="tower",
    )(
        request_slots.T, fetched.reshape(shards * capr, emb), cross_weight, cross_bias, tower_weight,
        tower_bias.reshape(1, -1), score_weight.reshape(1, -1),
    )
    return (new_table, new_accum.reshape(row_count), new_serving, scores.reshape(requests))


def solution(mesh):
    both = ("groups", "shard")
    in_specs = (
        P("shard", None), P("shard"), P("shard", None), P(both, None, None), P(both, None), P(both),
        P(both, None), P(both, None), P(), P(), P(), P(), P(),
    )
    out_specs = (P(both, None), P(both), P(both, None), P(both))
    return jax.shard_map(body, mesh=mesh, in_specs=in_specs, out_specs=out_specs, check_vma=False)
```

```python
import functools
import jax
import jax.numpy as jnp
from jax import lax
from jax.experimental import pallas as pl
from jax.experimental.pallas import tpu as pltpu
from jax.sharding import PartitionSpec as P

LEARN_RATE = 0.5
SCALE_FLOOR = 0.25
LANES = 128
DIGIT = 64
TILE = 256
BIG = 2048
MIB = 1024 * 1024


def ceil_to(value, unit):
    return -(-value // unit) * unit


SENDS = ((8,), (9, 1, 10), (2, 11, 3), (12, 4, 13), (5, 14, 6), (15, 7))
TAKES = ((8, 9, 1), (10, 2, 11), (3, 12, 4), (13, 5, 14))


def work(micros):
    return pl.CostEstimate(flops=0, transcendentals=0, bytes_accessed=int(micros * 3.0e6))


def pack_kernel(cap, req_rows, rows_hbm, ids_hbm, req_hbm, counts_ref, out_ref, ids_ref, req_ref, meta_ref, sems):
    f32 = jnp.float32
    loads = [
        pltpu.make_async_copy(ids_hbm, ids_ref, sems.at[0]),
        pltpu.make_async_copy(req_hbm, req_ref, sems.at[1]),
        pltpu.make_async_copy(rows_hbm, out_ref.at[:, :cap, :], sems.at[2]),
    ]
    for load in loads:
        load.start()
    meta_ref[...] = jnp.zeros_like(meta_ref)
    slot = lax.broadcasted_iota(jnp.int32, ids_ref.shape, 1)
    block = lax.broadcasted_iota(jnp.int32, ids_ref.shape, 0)
    count = jnp.zeros(ids_ref.shape, jnp.int32)
    for b in range(ids_ref.shape[0]):
        count = jnp.where(block == b, counts_ref[b], count)
    loads[0].wait()
    ids = ids_ref[...]
    width = ids.shape[1]
    meta_ref[:, 0, :width] = jnp.where(slot < count, ids // TILE, TILE - 1).astype(f32)
    meta_ref[:, 1, :width] = (ids % TILE).astype(f32)
    loads[1].wait()
    for row in range(req_rows):
        start = row * LANES
        stop = min(start + LANES, req_ref.shape[1])
        part = req_ref[:, start:stop]
        meta_ref[:, 2 + row, : stop - start] = (part // DIGIT).astype(f32)
        meta_ref[:, 2 + req_rows + row, : stop - start] = (part % DIGIT).astype(f32)
    out_ref[:, cap:, :] = meta_ref[...].astype(jnp.bfloat16)
    loads[2].wait()


def update_kernel(
    cap, req_at, req_rows, recv_ref, req_ref, accum_ref, item_hbm,
    table_hbm, accum_out, change_out, req_out, pair_ref, grad_ref, item_ref, table_out, sems,
):
    load_item = pltpu.make_async_copy(item_hbm, item_ref, sems.at[0])
    load_item.start()
    f32, bf16 = jnp.float32, jnp.bfloat16
    blocks = recv_ref.shape[0]
    row_count = item_hbm.shape[0]
    half_tiles = row_count // TILE // 2
    req_high = req_ref[:, req_at : req_at + req_rows, :].astype(f32)
    req_low = req_ref[:, req_at + req_rows : req_at + 2 * req_rows, :].astype(f32)
    req_out[...] = (req_high * DIGIT + req_low).astype(jnp.int32)
    eye = lax.broadcasted_iota(jnp.int32, (LANES, LANES), 0) == lax.broadcasted_iota(
        jnp.int32, (LANES, LANES), 1
    )
    eye_mark = jnp.where(eye, 1.0, 0.0).astype(bf16)
    ones = jnp.ones((LANES, LANES), bf16)
    keys = []
    for b in range(blocks):
        high = recv_ref[b, cap : cap + 1, :].astype(f32)
        low = recv_ref[b, cap + 1 : cap + 2, :].astype(f32)
        upper = high >= half_tiles
        keys.append((jnp.where(upper, high - half_tiles, high), low))
        spots = jnp.where(eye, jnp.where(upper, 1.0, 0.0), 0.0).astype(bf16)
        side = jnp.dot(spots, ones, preferred_element_type=f32)
        rows = recv_ref[b, :cap, :].astype(f32)
        pair_ref[b * cap : (b + 1) * cap, :LANES] = jnp.where(side > 0.5, 0.0, rows).astype(bf16)
        pair_ref[b * cap : (b + 1) * cap, LANES:] = jnp.where(side > 0.5, rows, 0.0).astype(bf16)
    row_in_tile = lax.broadcasted_iota(jnp.int32, (TILE, LANES), 0).astype(jnp.int16)
    mark, blank = jnp.ones((), bf16), jnp.zeros((), bf16)
    lines = lax.broadcasted_iota(jnp.int32, (8, LANES), 0)
    spread = jnp.where(lines == lax.broadcasted_iota(jnp.int32, (8, LANES), 1) // 32, 1.0, 0.0)
    spread = spread.astype(bf16)
    part = lax.broadcasted_iota(jnp.int32, (4 * LANES, LANES), 0)
    weigh = jnp.where(part < 2 * LANES, 1.0 / LANES, 1.0).astype(bf16)

    def scatter(t, carry):
        here = t.astype(f32)
        marks = []
        for high, low in keys:
            key = jnp.where(high == here, low, -1.0).astype(jnp.int16)
            marks.append(jnp.where(row_in_tile == jnp.broadcast_to(key, (TILE, LANES)), mark, blank))
        grad = jnp.dot(jnp.concatenate(marks, axis=1), pair_ref[...], preferred_element_type=f32)
        rows = pl.multiple_of(t * TILE, TILE)
        grad_ref[pl.ds(rows, TILE), :] = grad[:, :LANES]
        grad_ref[pl.ds(rows + row_count // 2, TILE), :] = grad[:, LANES:]
        return carry

    lax.fori_loop(0, half_tiles, scatter, 0, unroll=2)

    def adagrad(k, carry):
        rows = pl.ds(pl.multiple_of(k * BIG, BIG), BIG)
        grad = grad_ref[rows, :]
        square = grad * grad
        coarse = square.astype(bf16)
        rest = (square - coarse.astype(f32)).astype(bf16)
        lines = [accum_ref[pl.ds(k * (BIG // LANES) + q, 1), :] for q in range(BIG // LANES)]
        upper = [line.astype(bf16).astype(f32) for line in lines]
        olds = [
            jnp.concatenate([jnp.where(eye, line, 0.0) for line in part], axis=0).astype(bf16)
            for part in (upper, [line - high for line, high in zip(lines, upper)])
        ]
        accum = jnp.dot(
            jnp.concatenate([coarse, rest, *olds], axis=1), weigh, preferred_element_type=f32
        )
        for q in range(BIG // LANES):
            mine = jnp.where(eye, accum[q * LANES : (q + 1) * LANES], 0.0)
            accum_out[pl.ds(k * (BIG // LANES) + q, 1), :] = jnp.sum(mine, axis=0, keepdims=True)
        item = item_ref[rows, :].astype(f32)
        table_out[rows, :] = (item - LEARN_RATE * grad * lax.rsqrt(accum)).astype(bf16)
        return carry

    load_item.wait()
    lax.fori_loop(0, row_count // BIG, adagrad, 0)
    store_table = pltpu.make_async_copy(table_out, table_hbm, sems.at[1])
    store_table.start()

    def publish(k, carry):
        rows = pl.ds(pl.multiple_of(k * BIG, BIG), BIG)
        delta = table_out[rows, :].astype(f32) - item_ref[rows, :].astype(f32)
        turned = lax.dot_general(
            eye_mark, jnp.abs(delta).astype(bf16), (((1,), (1,)), ((), ())),
            preferred_element_type=f32,
        )
        top = jnp.max(turned.reshape(LANES // 32, 32, BIG), axis=1)
        top = jnp.concatenate([jnp.maximum(top, SCALE_FLOOR), jnp.zeros((4, BIG), f32)], axis=0)
        scale = lax.dot_general(
            top.astype(bf16), spread, (((0,), (0,)), ((), ())), preferred_element_type=f32
        )
        payload = (delta / scale).astype(bf16)
        change_out[rows, :] = payload.astype(f32) * scale
        return carry

    lax.fori_loop(0, row_count // BIG, publish, 0)
    store_table.wait()


def apply_kernel(change_ref, serving_ref, serving_out, live_out):
    f32 = jnp.float32
    serving = (serving_ref[...].astype(f32) + change_ref[...]).astype(jnp.bfloat16)
    serving_out[...] = serving
    live_out[...] = serving.astype(f32)


def unroll_of(width):
    for unroll in (64, 32, 16):
        if width % unroll == 0:
            return unroll
    return width


def copy_rows(from_ref, ids_ref, ids_at, to_ref, to_at, count):
    unroll = unroll_of(count)

    def some(k, carry):
        at = k * unroll
        rows = [from_ref[pl.ds(ids_ref[ids_at + at + u], 1), :] for u in range(unroll)]
        for u in range(unroll):
            to_ref[pl.ds(to_at + at + u, 1), :] = rows[u]
        return carry

    lax.fori_loop(0, count // unroll, some, 0)


def gather_kernel(moves, pitch, me_ref, ids_ref, live_ref, *outs):
    width = outs[0].shape[0]
    unroll = unroll_of(width)
    for move, out_ref in zip(moves, outs):
        start = lax.bitwise_xor(me_ref[0], move) * pitch

        def some(k, carry):
            at = start + k * unroll
            rows = [live_ref[pl.ds(ids_ref[at + u], 1), :] for u in range(unroll)]
            out_ref[pl.ds(pl.multiple_of(k * unroll, unroll), unroll), :] = jnp.concatenate(
                rows, axis=0
            ).astype(jnp.bfloat16)
            return carry

        lax.fori_loop(0, width // unroll, some, 0)


def gather_all_kernel(pitch, ids_ref, live_ref, out_ref):
    blocks, width, _ = out_ref.shape

    def block(b, carry):
        rows = [live_ref[pl.ds(ids_ref[b * pitch + u], 1), :] for u in range(width)]
        out_ref[b] = jnp.concatenate(rows, axis=0).astype(jnp.bfloat16)
        return carry

    lax.fori_loop(0, blocks, block, 0)


def token_kernel(token_ref, *refs):
    refs[-1][...] = token_ref[...]


def tower_kernel(
    moves, shape, pitch, token_ref, me_ref, ids_ref, slots_ref, live_ref, cross_hbm, cross_bias_ref, tower_hbm,
    tower_bias_ref, score_ref, serving_ref, *refs,
):
    f32, bf16 = jnp.float32, jnp.bfloat16
    feats, requests = shape
    pieces = refs[:-10]
    out_ref, serving_out, cross_ref, tower_ref, got_ref, served_ref = refs[-10:-4]
    wide_ref, plane_ref, crossed_ref, sems = refs[-4:]
    me = me_ref[0]
    loads = []
    for k, piece in enumerate(pieces):
        start, width = 0, piece.shape[0]
        if moves is not None:
            start = pl.multiple_of(lax.bitwise_xor(me, moves[k]) * width, width)
        loads.append(
            pltpu.make_async_copy(piece, got_ref.at[pl.ds(start, width), :], sems.at[4 + k])
        )
    load_cross = pltpu.make_async_copy(cross_hbm, cross_ref, sems.at[0])
    load_tower = pltpu.make_async_copy(tower_hbm, tower_ref, sems.at[1])
    load_serving = pltpu.make_async_copy(serving_ref, served_ref, sems.at[2])
    store_serving = pltpu.make_async_copy(served_ref, serving_out, sems.at[3])
    for load in loads:
        load.start()
    load_cross.start()
    load_serving.start()
    load_tower.start()
    for load in loads:
        load.wait()
    wide_ref[...] = got_ref[...].astype(f32)
    if moves is not None:
        width = pieces[0].shape[0]
        copy_rows(live_ref, ids_ref, me * pitch, wide_ref, me * width, width)
    load_serving.wait()
    store_serving.start()
    copy_rows(wide_ref, slots_ref, 0, plane_ref, 0, feats * requests)
    for f in range(feats):
        crossed_ref[:, f * LANES : (f + 1) * LANES] = plane_ref[
            f * requests : (f + 1) * requests, :
        ].astype(bf16)
    load_cross.wait()
    for layer in range(cross_ref.shape[0]):
        old = crossed_ref[...]
        projected = jnp.dot(old, cross_ref[layer], preferred_element_type=f32)
        projected = projected + cross_bias_ref[layer : layer + 1, :].astype(f32)
        for f in range(feats):
            cols = slice(f * LANES, (f + 1) * LANES)
            base = plane_ref[f * requests : (f + 1) * requests, :]
            crossed_ref[:, cols] = (base * projected[:, cols] + old[:, cols].astype(f32)).astype(bf16)
    load_tower.wait()
    hidden = tower_ref.shape[1]
    chunk = 1024
    total = jnp.zeros((requests, LANES), f32)
    for start in range(0, hidden, chunk):
        cols = slice(start, start + chunk)
        raw = jnp.dot(crossed_ref[...], tower_ref[:, cols], preferred_element_type=f32)
        raw = jnp.maximum(raw + tower_bias_ref[:, cols].astype(f32), 0.0)
        raw = raw * score_ref[:, cols].astype(f32)
        for q in range(chunk // LANES):
            total = total + raw[:, q * LANES : (q + 1) * LANES]
    eye = lax.broadcasted_iota(jnp.int32, (LANES, LANES), 0) == lax.broadcasted_iota(
        jnp.int32, (LANES, LANES), 1
    )
    for k in range(requests // LANES):
        column = jnp.sum(total[k * LANES : (k + 1) * LANES, :], axis=1, keepdims=True)
        out_ref[k : k + 1, :] = jnp.sum(jnp.where(eye, column, 0.0), axis=0, keepdims=True)
    store_serving.wait()


def body(
    item_table, row_accum, serving_table, grad_rows, grad_ids, grad_counts, request_ids,
    request_slots, cross_weight, cross_bias, tower_weight, tower_bias, score_weight,
):
    f32, bf16 = jnp.float32, jnp.bfloat16
    shards = lax.axis_size("shard")
    row_count, emb = item_table.shape
    cap, capr = grad_ids.shape[1], request_ids.shape[1]
    requests, feats = request_slots.shape
    req_rows = ceil_to(capr, LANES) // LANES
    meta_rows = ceil_to(2 + 2 * req_rows, 16)
    vmem = pl.BlockSpec(memory_space=pltpu.VMEM)
    smem = pl.BlockSpec(memory_space=pltpu.SMEM)
    hbm = pl.BlockSpec(memory_space=pltpu.HBM)

    def call(kernel, name, limit, **kwargs):
        params = pltpu.CompilerParams(vmem_limit_bytes=limit * MIB)
        return pl.pallas_call(kernel, name=name, compiler_params=params, **kwargs)

    packed = call(
        functools.partial(pack_kernel, cap, req_rows), "pack", 56,
        out_shape=jax.ShapeDtypeStruct((shards, cap + meta_rows, emb), bf16),
        in_specs=[hbm, hbm, hbm, smem],
        out_specs=vmem,
        scratch_shapes=[
            pltpu.VMEM((shards, cap), jnp.int32),
            pltpu.VMEM((shards, capr), jnp.int32),
            pltpu.VMEM((shards, meta_rows, LANES), f32),
            pltpu.SemaphoreType.DMA((3,)),
        ],
    )(grad_rows, grad_ids, request_ids, grad_counts)
    recv = lax.all_to_all(packed, "shard", split_axis=0, concat_axis=0, tiled=True)
    behind = [(i, (i - 1) % shards) for i in range(shards)]
    ahead = [(i, (i + 1) % shards) for i in range(shards)]
    serving_here = lax.ppermute(serving_table, "shard", behind)

    joined = recv
    if cap < LANES:
        groups = shards * cap // LANES
        marks = recv[:, cap : cap + 2, :cap].reshape(groups, LANES // cap, 2, cap)
        marks = marks.transpose(0, 2, 1, 3).reshape(groups, 2, LANES)
        marks = jnp.pad(marks, ((0, 0), (0, 14), (0, 0)))
        joined = jnp.concatenate([recv[:, :cap, :].reshape(groups, LANES, emb), marks], axis=1)

    new_table, new_accum, change, req = call(
        functools.partial(update_kernel, LANES, cap + 2, req_rows), "update", 32,
        out_shape=(
            jax.ShapeDtypeStruct((row_count, emb), bf16),
            jax.ShapeDtypeStruct((row_count // LANES, LANES), f32),
            jax.ShapeDtypeStruct((row_count, emb), f32),
            jax.ShapeDtypeStruct((shards, req_rows, LANES), jnp.int32),
        ),
        in_specs=[vmem, vmem, vmem, hbm],
        out_specs=(hbm, vmem, vmem, vmem),
        scratch_shapes=[
            pltpu.VMEM((shards * cap, 2 * LANES), bf16),
            pltpu.VMEM((row_count, LANES), f32),
            pltpu.VMEM((row_count, LANES), bf16),
            pltpu.VMEM((row_count, LANES), bf16),
            pltpu.SemaphoreType.DMA((2,)),
        ],
    )(joined, recv, row_accum.reshape(-1, LANES), item_table)
    serving_next, live = call(
        apply_kernel, "apply", 8,
        out_shape=(
            jax.ShapeDtypeStruct((row_count, emb), bf16),
            jax.ShapeDtypeStruct((row_count, emb), f32),
        ),
        in_specs=[vmem, vmem],
        out_specs=(vmem, vmem),
    )(change, serving_here)
    req = req.reshape(-1)

    me = lax.axis_index("shard").astype(jnp.int32).reshape(1)
    pitch = req_rows * LANES
    sent = lax.ppermute(serving_next, "shard", ahead)
    if shards == 16:
        moves, pieces = [], []
        for sends in SENDS:
            found = call(
                functools.partial(gather_kernel, sends, pitch), "gather", 4,
                out_shape=(jax.ShapeDtypeStruct((capr, emb), bf16),) * len(sends),
                in_specs=[smem, smem, vmem],
                out_specs=(vmem,) * len(sends),
                cost_estimate=work(0.6 * len(sends)),
            )(me, req, live)
            for move, rows in zip(sends, found):
                moves.append(move)
                pieces.append(lax.ppermute(rows, "shard", [(i, i ^ move) for i in range(shards)]))
        token = jnp.zeros((8, LANES), f32)
        for takes in TAKES:
            token = call(
                token_kernel, "token", 4,
                out_shape=jax.ShapeDtypeStruct((8, LANES), f32),
                in_specs=[vmem] + [hbm] * len(takes),
                out_specs=vmem,
                cost_estimate=work(0.6 * len(takes) + 0.6),
            )(token, *[pieces[moves.index(move)] for move in takes])
    else:
        found = call(
            functools.partial(gather_all_kernel, pitch), "gather", 8,
            out_shape=jax.ShapeDtypeStruct((shards, capr, emb), bf16),
            in_specs=[smem, vmem],
            out_specs=vmem,
        )(req, live)
        moves, token = None, jnp.zeros((8, LANES), f32)
        got = lax.all_to_all(found, "shard", split_axis=0, concat_axis=0, tiled=True)
        pieces = [got.reshape(shards * capr, emb)]
    scores, new_serving = call(
        functools.partial(tower_kernel, moves, (feats, requests), pitch), "tower", 58,
        out_shape=(
            jax.ShapeDtypeStruct((requests // LANES, LANES), f32),
            jax.ShapeDtypeStruct((row_count, emb), bf16),
        ),
        in_specs=[vmem] + [smem] * 3 + [vmem, hbm, vmem, hbm, vmem, vmem, hbm] + [hbm] * len(pieces),
        out_specs=(vmem, hbm),
        scratch_shapes=[
            pltpu.VMEM(cross_weight.shape, bf16),
            pltpu.VMEM(tower_weight.shape, bf16),
            pltpu.VMEM((shards * capr, emb), bf16),
            pltpu.VMEM((row_count, emb), bf16),
            pltpu.VMEM((shards * capr, emb), f32),
            pltpu.VMEM((feats * requests, emb), f32),
            pltpu.VMEM((requests, feats * emb), bf16),
            pltpu.SemaphoreType.DMA((4 + len(pieces),)),
        ],
    )(
        token, me, req, request_slots.T.reshape(-1), live, cross_weight, cross_bias, tower_weight,
        tower_bias.reshape(1, -1), score_weight.reshape(1, -1), sent, *pieces,
    )
    return (new_table, new_accum.reshape(row_count), new_serving, scores.reshape(requests))


def solution(mesh):
    both = ("groups", "shard")
    in_specs = (
        P("shard", None), P("shard"), P("shard", None), P(both, None, None), P(both, None), P(both),
        P(both, None), P(both, None), P(), P(), P(), P(), P(),
    )
    out_specs = (P(both, None), P(both), P(both, None), P(both))
    return jax.shard_map(body, mesh=mesh, in_specs=in_specs, out_specs=out_specs, check_vma=False)
```

```python
import functools
import jax
import jax.numpy as jnp
from jax import lax
from jax.experimental import pallas as pl
from jax.experimental.pallas import tpu as pltpu
from jax.sharding import PartitionSpec as P

LEARN_RATE = 0.5
SCALE_FLOOR = 0.25
LANES = 128
DIGIT = 64
TILE = 256
BIG = 2048
MIB = 1024 * 1024


def ceil_to(value, unit):
    return -(-value // unit) * unit


SENDS = ((8,), (9, 1, 10), (2, 11, 3), (12, 4, 13), (5, 14, 6), (15, 7, 0))
TAKES = ((8, 9, 1), (10, 2, 11), (3, 12, 4), (13, 5, 14))
FAR = ((7, 8), (15, 0))


def work(micros):
    return pl.CostEstimate(flops=0, transcendentals=0, bytes_accessed=int(micros * 3.0e6))


def pack_kernel(
    cap, req_rows, rows_hbm, ids_hbm, req_hbm, serving_hbm, counts_ref, out_ref, aside_ref,
    ids_ref, req_ref, meta_ref, sems,
):
    f32 = jnp.float32
    half = aside_ref.shape[0]
    loads = [
        pltpu.make_async_copy(ids_hbm, ids_ref, sems.at[0]),
        pltpu.make_async_copy(req_hbm, req_ref, sems.at[1]),
        pltpu.make_async_copy(rows_hbm, out_ref.at[:, :cap, :], sems.at[2]),
        pltpu.make_async_copy(serving_hbm.at[pl.ds(half, half), :], aside_ref, sems.at[3]),
    ]
    for load in loads:
        load.start()
    meta_ref[...] = jnp.zeros_like(meta_ref)
    slot = lax.broadcasted_iota(jnp.int32, ids_ref.shape, 1)
    block = lax.broadcasted_iota(jnp.int32, ids_ref.shape, 0)
    count = jnp.zeros(ids_ref.shape, jnp.int32)
    for b in range(ids_ref.shape[0]):
        count = jnp.where(block == b, counts_ref[b], count)
    loads[0].wait()
    ids = ids_ref[...]
    width = ids.shape[1]
    meta_ref[:, 0, :width] = jnp.where(slot < count, ids // TILE, TILE - 1).astype(f32)
    meta_ref[:, 1, :width] = (ids % TILE).astype(f32)
    loads[1].wait()
    for row in range(req_rows):
        start = row * LANES
        stop = min(start + LANES, req_ref.shape[1])
        part = req_ref[:, start:stop]
        meta_ref[:, 2 + row, : stop - start] = (part // DIGIT).astype(f32)
        meta_ref[:, 2 + req_rows + row, : stop - start] = (part % DIGIT).astype(f32)
    out_ref[:, cap:, :] = meta_ref[...].astype(jnp.bfloat16)
    loads[2].wait()
    loads[3].wait()


def update_kernel(
    cap, req_at, req_rows, recv_ref, req_ref, accum_ref, item_hbm,
    table_hbm, accum_out, change_out, req_out, pair_ref, grad_ref, item_ref, table_out, sems,
):
    load_item = pltpu.make_async_copy(item_hbm, item_ref, sems.at[0])
    load_item.start()
    f32, bf16 = jnp.float32, jnp.bfloat16
    blocks = recv_ref.shape[0]
    row_count = item_hbm.shape[0]
    half_tiles = row_count // TILE // 2
    req_high = req_ref[:, req_at : req_at + req_rows, :].astype(f32)
    req_low = req_ref[:, req_at + req_rows : req_at + 2 * req_rows, :].astype(f32)
    req_out[...] = (req_high * DIGIT + req_low).astype(jnp.int32)
    eye = lax.broadcasted_iota(jnp.int32, (LANES, LANES), 0) == lax.broadcasted_iota(
        jnp.int32, (LANES, LANES), 1
    )
    eye_mark = jnp.where(eye, 1.0, 0.0).astype(bf16)
    ones = jnp.ones((LANES, LANES), bf16)
    keys = []
    for b in range(blocks):
        high = recv_ref[b, cap : cap + 1, :].astype(f32)
        low = recv_ref[b, cap + 1 : cap + 2, :].astype(f32)
        upper = high >= half_tiles
        keys.append((jnp.where(upper, high - half_tiles, high), low))
        spots = jnp.where(eye, jnp.where(upper, 1.0, 0.0), 0.0).astype(bf16)
        side = jnp.dot(spots, ones, preferred_element_type=f32)
        rows = recv_ref[b, :cap, :].astype(f32)
        pair_ref[b * cap : (b + 1) * cap, :LANES] = jnp.where(side > 0.5, 0.0, rows).astype(bf16)
        pair_ref[b * cap : (b + 1) * cap, LANES:] = jnp.where(side > 0.5, rows, 0.0).astype(bf16)
    row_in_tile = lax.broadcasted_iota(jnp.int32, (TILE, LANES), 0).astype(jnp.int16)
    mark, blank = jnp.ones((), bf16), jnp.zeros((), bf16)
    lines = lax.broadcasted_iota(jnp.int32, (8, LANES), 0)
    spread = jnp.where(lines == lax.broadcasted_iota(jnp.int32, (8, LANES), 1) // 32, 1.0, 0.0)
    spread = spread.astype(bf16)
    part = lax.broadcasted_iota(jnp.int32, (4 * LANES, LANES), 0)
    weigh = jnp.where(part < 2 * LANES, 1.0 / LANES, 1.0).astype(bf16)

    def scatter(t, carry):
        here = t.astype(f32)
        marks = []
        for high, low in keys:
            key = jnp.where(high == here, low, -1.0).astype(jnp.int16)
            marks.append(jnp.where(row_in_tile == jnp.broadcast_to(key, (TILE, LANES)), mark, blank))
        grad = jnp.dot(jnp.concatenate(marks, axis=1), pair_ref[...], preferred_element_type=f32)
        rows = pl.multiple_of(t * TILE, TILE)
        grad_ref[pl.ds(rows, TILE), :] = grad[:, :LANES]
        grad_ref[pl.ds(rows + row_count // 2, TILE), :] = grad[:, LANES:]
        return carry

    lax.fori_loop(0, half_tiles, scatter, 0, unroll=2)

    def adagrad(k, carry):
        rows = pl.ds(pl.multiple_of(k * BIG, BIG), BIG)
        grad = grad_ref[rows, :]
        square = grad * grad
        coarse = square.astype(bf16)
        rest = (square - coarse.astype(f32)).astype(bf16)
        lines = [accum_ref[pl.ds(k * (BIG // LANES) + q, 1), :] for q in range(BIG // LANES)]
        upper = [line.astype(bf16).astype(f32) for line in lines]
        olds = [
            jnp.concatenate([jnp.where(eye, line, 0.0) for line in part], axis=0).astype(bf16)
            for part in (upper, [line - high for line, high in zip(lines, upper)])
        ]
        accum = jnp.dot(
            jnp.concatenate([coarse, rest, *olds], axis=1), weigh, preferred_element_type=f32
        )
        for q in range(BIG // LANES):
            mine = jnp.where(eye, accum[q * LANES : (q + 1) * LANES], 0.0)
            accum_out[pl.ds(k * (BIG // LANES) + q, 1), :] = jnp.sum(mine, axis=0, keepdims=True)
        item = item_ref[rows, :].astype(f32)
        table_out[rows, :] = (item - LEARN_RATE * grad * lax.rsqrt(accum)).astype(bf16)
        return carry

    load_item.wait()
    lax.fori_loop(0, row_count // BIG, adagrad, 0)
    store_table = pltpu.make_async_copy(table_out, table_hbm, sems.at[1])
    store_table.start()

    def publish(k, carry):
        rows = pl.ds(pl.multiple_of(k * BIG, BIG), BIG)
        delta = table_out[rows, :].astype(f32) - item_ref[rows, :].astype(f32)
        turned = lax.dot_general(
            eye_mark, jnp.abs(delta).astype(bf16), (((1,), (1,)), ((), ())),
            preferred_element_type=f32,
        )
        top = jnp.max(turned.reshape(LANES // 32, 32, BIG), axis=1)
        top = jnp.concatenate([jnp.maximum(top, SCALE_FLOOR), jnp.zeros((4, BIG), f32)], axis=0)
        scale = lax.dot_general(
            top.astype(bf16), spread, (((0,), (0,)), ((), ())), preferred_element_type=f32
        )
        payload = (delta / scale).astype(bf16)
        change_out[rows, :] = payload.astype(f32) * scale
        return carry

    lax.fori_loop(0, row_count // BIG, publish, 0)
    store_table.wait()


def stage_kernel(serving_hbm, *refs):
    out_ref, sem = refs[-2:]
    load = pltpu.make_async_copy(serving_hbm.at[pl.ds(0, out_ref.shape[0]), :], out_ref, sem)
    load.start()
    load.wait()


def apply_kernel(me_ref, change_ref, upper_ref, lower_ref, around_ref, serving_out, live_out):
    f32 = jnp.float32
    half = upper_ref.shape[0]
    turned = lax.rem(me_ref[0], 4) == 3
    lower = jnp.where(turned, around_ref[...].astype(f32), lower_ref[...].astype(f32))
    for start, old in ((0, upper_ref[...].astype(f32)), (half, lower)):
        serving = (old + change_ref[start : start + half, :]).astype(jnp.bfloat16)
        serving_out[start : start + half, :] = serving
        live_out[start : start + half, :] = serving.astype(f32)


def unroll_of(width):
    for unroll in (64, 32, 16):
        if width % unroll == 0:
            return unroll
    return width


def gather_kernel(moves, pitch, me_ref, ids_ref, live_ref, *outs):
    width = outs[0].shape[0]
    unroll = unroll_of(width)
    for move, out_ref in zip(moves, outs):
        start = lax.bitwise_xor(me_ref[0], move) * pitch

        def some(k, carry):
            at = start + k * unroll
            rows = [live_ref[pl.ds(ids_ref[at + u], 1), :] for u in range(unroll)]
            out_ref[pl.ds(pl.multiple_of(k * unroll, unroll), unroll), :] = jnp.concatenate(
                rows, axis=0
            ).astype(jnp.bfloat16)
            return carry

        lax.fori_loop(0, width // unroll, some, 0)


def gather_all_kernel(pitch, ids_ref, live_ref, out_ref):
    blocks, width, _ = out_ref.shape

    def block(b, carry):
        rows = [live_ref[pl.ds(ids_ref[b * pitch + u], 1), :] for u in range(width)]
        out_ref[b] = jnp.concatenate(rows, axis=0).astype(jnp.bfloat16)
        return carry

    lax.fori_loop(0, blocks, block, 0)


def hold_kernel(live_ref, *refs):
    refs[-1][...] = live_ref[...].astype(jnp.bfloat16)


def deliver_kernel(every, me_ref, far_ref, near_hbm, out_hbm, sem):
    @pl.when(lax.rem(me_ref[0], every) == 0)
    def _():
        store = pltpu.make_async_copy(far_ref, out_hbm, sem)
        store.start()
        store.wait()


def token_kernel(token_ref, *refs):
    refs[-1][...] = token_ref[...]


def tower_kernel(
    moves, shape, token_ref, me_ref, slots_ref, cross_hbm, cross_bias_ref, tower_hbm,
    tower_bias_ref, score_ref, serving_ref, *refs,
):
    f32, bf16 = jnp.float32, jnp.bfloat16
    feats, requests = shape
    pieces = refs[:-11]
    out_ref, serving_out, cross_ref, tower_ref, got_ref, served_ref = refs[-11:-5]
    wide_ref, plane_a, plane_b, crossed_ref, sems = refs[-5:]
    planes = (plane_a, plane_b)
    me = me_ref[0]
    loads = []
    for k, piece in enumerate(pieces):
        start, width = 0, piece.shape[0]
        if moves is not None:
            start = pl.multiple_of(lax.bitwise_xor(me, moves[k]) * width, width)
        loads.append(
            pltpu.make_async_copy(piece, got_ref.at[pl.ds(start, width), :], sems.at[4 + k])
        )
    load_cross = pltpu.make_async_copy(cross_hbm, cross_ref, sems.at[0])
    load_tower = pltpu.make_async_copy(tower_hbm, tower_ref, sems.at[1])
    load_serving = pltpu.make_async_copy(serving_ref, served_ref, sems.at[2])
    store_serving = pltpu.make_async_copy(served_ref, serving_out, sems.at[3])
    for load in loads:
        load.start()
    load_cross.start()
    load_serving.start()
    load_tower.start()
    for load in loads:
        load.wait()
    wide_ref[...] = got_ref[...].astype(f32)
    load_serving.wait()
    store_serving.start()
    chunk = 256
    batch = 64

    def collect(c):
        plane = planes[c % 2]
        for f in range(feats):
            for r in range(0, chunk, batch):
                at = f * requests + c * chunk + r
                rows = [wide_ref[pl.ds(slots_ref[at + u], 1), :] for u in range(batch)]
                for u in range(batch):
                    plane[f * chunk + r + u : f * chunk + r + u + 1, :] = rows[u]
                yield

    for _ in collect(0):
        pass
    load_cross.wait()
    layers = cross_ref.shape[0]
    for c in range(requests // chunk):
        plane = planes[c % 2]
        base = jnp.concatenate([plane[f * chunk : (f + 1) * chunk, :] for f in range(feats)], axis=1)
        coming = list(range(feats * chunk // batch)) if (c + 1) * chunk < requests else []
        batches = collect(c + 1) if coming else iter(())
        old = base.astype(bf16)
        for layer in range(layers):
            projected = jnp.dot(old, cross_ref[layer], preferred_element_type=f32)
            for _ in coming[layer::layers]:
                next(batches)
            projected = projected + cross_bias_ref[layer : layer + 1, :].astype(f32)
            old = (base * projected + old.astype(f32)).astype(bf16)
        crossed_ref[c * chunk : (c + 1) * chunk, :] = old
    load_tower.wait()
    hidden = tower_ref.shape[1]
    chunk = 1024
    total = jnp.zeros((requests, LANES), f32)
    for start in range(0, hidden, chunk):
        cols = slice(start, start + chunk)
        raw = jnp.dot(crossed_ref[...], tower_ref[:, cols], preferred_element_type=f32)
        raw = jnp.maximum(raw + tower_bias_ref[:, cols].astype(f32), 0.0)
        raw = raw * score_ref[:, cols].astype(f32)
        for q in range(chunk // LANES):
            total = total + raw[:, q * LANES : (q + 1) * LANES]
    eye = lax.broadcasted_iota(jnp.int32, (LANES, LANES), 0) == lax.broadcasted_iota(
        jnp.int32, (LANES, LANES), 1
    )
    for k in range(requests // LANES):
        column = jnp.sum(total[k * LANES : (k + 1) * LANES, :], axis=1, keepdims=True)
        out_ref[k : k + 1, :] = jnp.sum(jnp.where(eye, column, 0.0), axis=0, keepdims=True)
    store_serving.wait()


def body(
    item_table, row_accum, serving_table, grad_rows, grad_ids, grad_counts, request_ids,
    request_slots, cross_weight, cross_bias, tower_weight, tower_bias, score_weight,
):
    f32, bf16 = jnp.float32, jnp.bfloat16
    shards = lax.axis_size("shard")
    row_count, emb = item_table.shape
    cap, capr = grad_ids.shape[1], request_ids.shape[1]
    requests, feats = request_slots.shape
    req_rows = ceil_to(capr, LANES) // LANES
    meta_rows = ceil_to(2 + 2 * req_rows, 16)
    vmem = pl.BlockSpec(memory_space=pltpu.VMEM)
    smem = pl.BlockSpec(memory_space=pltpu.SMEM)
    hbm = pl.BlockSpec(memory_space=pltpu.HBM)

    def call(kernel, name, limit, **kwargs):
        params = pltpu.CompilerParams(vmem_limit_bytes=limit * MIB)
        return pl.pallas_call(kernel, name=name, compiler_params=params, **kwargs)

    me = lax.axis_index("shard").astype(jnp.int32).reshape(1)

    packed, aside = call(
        functools.partial(pack_kernel, cap, req_rows), "pack", 56,
        out_shape=(
            jax.ShapeDtypeStruct((shards, cap + meta_rows, emb), bf16),
            jax.ShapeDtypeStruct((row_count // 2, emb), bf16),
        ),
        in_specs=[hbm] * 4 + [smem],
        out_specs=(vmem, vmem),
        scratch_shapes=[
            pltpu.VMEM((shards, cap), jnp.int32),
            pltpu.VMEM((shards, capr), jnp.int32),
            pltpu.VMEM((shards, meta_rows, LANES), f32),
            pltpu.SemaphoreType.DMA((4,)),
        ],
    )(grad_rows, grad_ids, request_ids, serving_table, grad_counts)
    recv = lax.all_to_all(packed, "shard", split_axis=0, concat_axis=0, tiled=True)
    behind = [(i, (i - 1) % shards) for i in range(shards)]
    ahead = [(i, (i + 1) % shards) for i in range(shards)]
    slots = request_slots.T.reshape(-1)
    tower_bias, score_weight = tower_bias.reshape(1, -1), score_weight.reshape(1, -1)
    half = row_count // 2
    if shards == 16:
        straight = [(i, i - 1) for i in range(shards) if i % 4]
        lower = lax.ppermute(aside, "shard", straight + [(i, i + 3) for i in range(0, shards, 4)])
        upper = call(
            stage_kernel, "stage", 8,
            out_shape=jax.ShapeDtypeStruct((half, emb), bf16),
            in_specs=[hbm] * 5,
            out_specs=vmem,
            scratch_shapes=[pltpu.SemaphoreType.DMA],
            cost_estimate=work(1.0),
        )(serving_table, lower, slots, tower_bias, score_weight)
        upper = lax.ppermute(upper, "shard", behind)
        around = lax.ppermute(lower, "shard", [(3, 15), (7, 3), (11, 7), (15, 11)])
        serving_parts = (upper, lower, around)
    else:
        serving_here = lax.ppermute(serving_table, "shard", behind)
        serving_parts = (serving_here[:half], serving_here[half:], serving_here[half:])

    joined = recv
    if cap < LANES:
        groups = shards * cap // LANES
        marks = recv[:, cap : cap + 2, :cap].reshape(groups, LANES // cap, 2, cap)
        marks = marks.transpose(0, 2, 1, 3).reshape(groups, 2, LANES)
        marks = jnp.pad(marks, ((0, 0), (0, 14), (0, 0)))
        joined = jnp.concatenate([recv[:, :cap, :].reshape(groups, LANES, emb), marks], axis=1)

    new_table, new_accum, change, req = call(
        functools.partial(update_kernel, LANES, cap + 2, req_rows), "update", 32,
        out_shape=(
            jax.ShapeDtypeStruct((row_count, emb), bf16),
            jax.ShapeDtypeStruct((row_count // LANES, LANES), f32),
            jax.ShapeDtypeStruct((row_count, emb), f32),
            jax.ShapeDtypeStruct((shards, req_rows, LANES), jnp.int32),
        ),
        in_specs=[vmem, vmem, vmem, hbm],
        out_specs=(hbm, vmem, vmem, vmem),
        scratch_shapes=[
            pltpu.VMEM((shards * cap, 2 * LANES), bf16),
            pltpu.VMEM((row_count, LANES), f32),
            pltpu.VMEM((row_count, LANES), bf16),
            pltpu.VMEM((row_count, LANES), bf16),
            pltpu.SemaphoreType.DMA((2,)),
        ],
    )(joined, recv, row_accum.reshape(-1, LANES), item_table)
    serving_next, live = call(
        apply_kernel, "apply", 8,
        out_shape=(
            jax.ShapeDtypeStruct((row_count, emb), bf16),
            jax.ShapeDtypeStruct((row_count, emb), f32),
        ),
        in_specs=[smem] + [vmem] * 4,
        out_specs=(vmem, vmem),
    )(me, change, *serving_parts)
    req = req.reshape(-1)

    pitch = req_rows * LANES
    far = FAR if shards == 16 else ()
    sent = lax.ppermute(serving_next, "shard", [pair for pair in ahead if pair not in far])
    if shards == 16:
        moves, pieces = [], []
        for sends in SENDS:
            found = call(
                functools.partial(gather_kernel, sends, pitch), "gather", 4,
                out_shape=(jax.ShapeDtypeStruct((capr, emb), bf16),) * len(sends),
                in_specs=[smem, smem, vmem],
                out_specs=(vmem,) * len(sends),
                cost_estimate=work(0.6 * len(sends)),
            )(me, req, live)
            for move, rows in zip(sends, found):
                moves.append(move)
                if move == 0:
                    pieces.append(rows)
                    continue
                pieces.append(lax.ppermute(rows, "shard", [(i, i ^ move) for i in range(shards)]))
        token = jnp.zeros((8, LANES), f32)
        for takes in TAKES:
            token = call(
                token_kernel, "token", 4,
                out_shape=jax.ShapeDtypeStruct((8, LANES), f32),
                in_specs=[vmem] + [hbm] * len(takes),
                out_specs=vmem,
                cost_estimate=work(0.6 * len(takes) + 0.6),
            )(token, *[pieces[moves.index(move)] for move in takes])
        held = call(
            hold_kernel, "hold", 8,
            out_shape=jax.ShapeDtypeStruct((row_count, emb), bf16),
            in_specs=[vmem] + [hbm] * len(pieces),
            out_specs=vmem,
            cost_estimate=work(0.5),
        )(live, *pieces)
        sent_far = lax.ppermute(held, "shard", far)
    else:
        found = call(
            functools.partial(gather_all_kernel, pitch), "gather", 8,
            out_shape=jax.ShapeDtypeStruct((shards, capr, emb), bf16),
            in_specs=[smem, vmem],
            out_specs=vmem,
        )(req, live)
        moves, token = None, jnp.zeros((8, LANES), f32)
        got = lax.all_to_all(found, "shard", split_axis=0, concat_axis=0, tiled=True)
        pieces = [got.reshape(shards * capr, emb)]
    scores, new_serving = call(
        functools.partial(tower_kernel, moves, (feats, requests)), "tower", 58,
        out_shape=(
            jax.ShapeDtypeStruct((requests // LANES, LANES), f32),
            jax.ShapeDtypeStruct((row_count, emb), bf16),
        ),
        in_specs=[vmem] + [smem] * 2 + [hbm, vmem, hbm, vmem, vmem, hbm] + [hbm] * len(pieces),
        out_specs=(vmem, hbm),
        scratch_shapes=[
            pltpu.VMEM(cross_weight.shape, bf16),
            pltpu.VMEM(tower_weight.shape, bf16),
            pltpu.VMEM((shards * capr, emb), bf16),
            pltpu.VMEM((row_count, emb), bf16),
            pltpu.VMEM((shards * capr, emb), f32),
            pltpu.VMEM((feats * 256, emb), f32),
            pltpu.VMEM((feats * 256, emb), f32),
            pltpu.VMEM((requests, feats * emb), bf16),
            pltpu.SemaphoreType.DMA((4 + len(pieces),)),
        ],
    )(
        token, me, slots, cross_weight, cross_bias, tower_weight,
        tower_bias, score_weight, sent, *pieces,
    )
    if far:
        new_serving = call(
            functools.partial(deliver_kernel, shards // 2), "deliver", 8,
            out_shape=jax.ShapeDtypeStruct((row_count, emb), bf16),
            in_specs=[smem, vmem, hbm],
            out_specs=hbm,
            scratch_shapes=[pltpu.SemaphoreType.DMA],
            input_output_aliases={2: 0},
        )(me, sent_far, new_serving)
    return (new_table, new_accum.reshape(row_count), new_serving, scores.reshape(requests))


def solution(mesh):
    both = ("groups", "shard")
    in_specs = (
        P("shard", None), P("shard"), P("shard", None), P(both, None, None), P(both, None), P(both),
        P(both, None), P(both, None), P(), P(), P(), P(), P(),
    )
    out_specs = (P(both, None), P(both), P(both, None), P(both))
    return jax.shard_map(body, mesh=mesh, in_specs=in_specs, out_specs=out_specs, check_vma=False)
```

```python
import functools
import jax
import jax.numpy as jnp
from jax import lax
from jax.experimental import pallas as pl
from jax.experimental.pallas import tpu as pltpu
from jax.sharding import PartitionSpec as P

LEARN_RATE = 0.5
SCALE_FLOOR = 0.25
LANES = 128
DIGIT = 64
TILE = 256
BIG = 2048
MIB = 1024 * 1024


def ceil_to(value, unit):
    return -(-value // unit) * unit


SENDS = ((8,), (9, 1, 10), (2, 11, 3), (12, 4, 13), (5, 14, 6), (15, 7, 0))
TAKES = ((8, 9, 1), (10, 2, 11), (3, 12, 4), (13, 5, 14))


def work(micros):
    return pl.CostEstimate(flops=0, transcendentals=0, bytes_accessed=int(micros * 3.0e6))


def pack_kernel(
    cap, req_rows, rows_hbm, ids_hbm, req_hbm, serving_hbm, counts_ref, out_ref, aside_ref,
    ids_ref, req_ref, meta_ref, sems,
):
    f32 = jnp.float32
    half = aside_ref.shape[0]
    loads = [
        pltpu.make_async_copy(ids_hbm, ids_ref, sems.at[0]),
        pltpu.make_async_copy(req_hbm, req_ref, sems.at[1]),
        pltpu.make_async_copy(rows_hbm, out_ref.at[:, :cap, :], sems.at[2]),
        pltpu.make_async_copy(serving_hbm.at[pl.ds(half, half), :], aside_ref, sems.at[3]),
    ]
    for load in loads:
        load.start()
    meta_ref[...] = jnp.zeros_like(meta_ref)
    slot = lax.broadcasted_iota(jnp.int32, ids_ref.shape, 1)
    block = lax.broadcasted_iota(jnp.int32, ids_ref.shape, 0)
    count = jnp.zeros(ids_ref.shape, jnp.int32)
    for b in range(ids_ref.shape[0]):
        count = jnp.where(block == b, counts_ref[b], count)
    loads[0].wait()
    ids = ids_ref[...]
    width = ids.shape[1]
    meta_ref[:, 0, :width] = jnp.where(slot < count, ids // TILE, TILE - 1).astype(f32)
    meta_ref[:, 1, :width] = (ids % TILE).astype(f32)
    loads[1].wait()
    for row in range(req_rows):
        start = row * LANES
        stop = min(start + LANES, req_ref.shape[1])
        part = req_ref[:, start:stop]
        meta_ref[:, 2 + row, : stop - start] = (part // DIGIT).astype(f32)
        meta_ref[:, 2 + req_rows + row, : stop - start] = (part % DIGIT).astype(f32)
    out_ref[:, cap:, :] = meta_ref[...].astype(jnp.bfloat16)
    loads[2].wait()
    loads[3].wait()


def update_kernel(
    cap, req_at, req_rows, recv_ref, req_ref, accum_ref, item_hbm,
    table_hbm, accum_out, change_out, req_out, pair_ref, grad_ref, item_ref, table_out, sems,
):
    load_item = pltpu.make_async_copy(item_hbm, item_ref, sems.at[0])
    load_item.start()
    f32, bf16 = jnp.float32, jnp.bfloat16
    blocks = recv_ref.shape[0]
    row_count = item_hbm.shape[0]
    half_tiles = row_count // TILE // 2
    req_high = req_ref[:, req_at : req_at + req_rows, :].astype(f32)
    req_low = req_ref[:, req_at + req_rows : req_at + 2 * req_rows, :].astype(f32)
    req_out[...] = (req_high * DIGIT + req_low).astype(jnp.int32)
    eye = lax.broadcasted_iota(jnp.int32, (LANES, LANES), 0) == lax.broadcasted_iota(
        jnp.int32, (LANES, LANES), 1
    )
    eye_mark = jnp.where(eye, 1.0, 0.0).astype(bf16)
    ones = jnp.ones((LANES, LANES), bf16)
    keys = []
    for b in range(blocks):
        high = recv_ref[b, cap : cap + 1, :].astype(f32)
        low = recv_ref[b, cap + 1 : cap + 2, :].astype(f32)
        upper = high >= half_tiles
        keys.append((jnp.where(upper, high - half_tiles, high), low))
        spots = jnp.where(eye, jnp.where(upper, 1.0, 0.0), 0.0).astype(bf16)
        side = jnp.dot(spots, ones, preferred_element_type=f32)
        rows = recv_ref[b, :cap, :].astype(f32)
        pair_ref[b * cap : (b + 1) * cap, :LANES] = jnp.where(side > 0.5, 0.0, rows).astype(bf16)
        pair_ref[b * cap : (b + 1) * cap, LANES:] = jnp.where(side > 0.5, rows, 0.0).astype(bf16)
    row_in_tile = lax.broadcasted_iota(jnp.int32, (TILE, LANES), 0).astype(jnp.int16)
    mark, blank = jnp.ones((), bf16), jnp.zeros((), bf16)
    lines = lax.broadcasted_iota(jnp.int32, (8, LANES), 0)
    spread = jnp.where(lines == lax.broadcasted_iota(jnp.int32, (8, LANES), 1) // 32, 1.0, 0.0)
    spread = spread.astype(bf16)
    part = lax.broadcasted_iota(jnp.int32, (4 * LANES, LANES), 0)
    weigh = jnp.where(part < 2 * LANES, 1.0 / LANES, 1.0).astype(bf16)

    def scatter(t, carry):
        here = t.astype(f32)
        marks = []
        for high, low in keys:
            key = jnp.where(high == here, low, -1.0).astype(jnp.int16)
            marks.append(jnp.where(row_in_tile == jnp.broadcast_to(key, (TILE, LANES)), mark, blank))
        grad = jnp.dot(jnp.concatenate(marks, axis=1), pair_ref[...], preferred_element_type=f32)
        rows = pl.multiple_of(t * TILE, TILE)
        grad_ref[pl.ds(rows, TILE), :] = grad[:, :LANES]
        grad_ref[pl.ds(rows + row_count // 2, TILE), :] = grad[:, LANES:]
        return carry

    lax.fori_loop(0, half_tiles, scatter, 0, unroll=2)

    def adagrad(k, carry):
        rows = pl.ds(pl.multiple_of(k * BIG, BIG), BIG)
        grad = grad_ref[rows, :]
        square = grad * grad
        coarse = square.astype(bf16)
        rest = (square - coarse.astype(f32)).astype(bf16)
        lines = [accum_ref[pl.ds(k * (BIG // LANES) + q, 1), :] for q in range(BIG // LANES)]
        upper = [line.astype(bf16).astype(f32) for line in lines]
        olds = [
            jnp.concatenate([jnp.where(eye, line, 0.0) for line in part], axis=0).astype(bf16)
            for part in (upper, [line - high for line, high in zip(lines, upper)])
        ]
        accum = jnp.dot(
            jnp.concatenate([coarse, rest, *olds], axis=1), weigh, preferred_element_type=f32
        )
        for q in range(BIG // LANES):
            mine = jnp.where(eye, accum[q * LANES : (q + 1) * LANES], 0.0)
            accum_out[pl.ds(k * (BIG // LANES) + q, 1), :] = jnp.sum(mine, axis=0, keepdims=True)
        item = item_ref[rows, :].astype(f32)
        table_out[rows, :] = (item - LEARN_RATE * grad * lax.rsqrt(accum)).astype(bf16)
        return carry

    load_item.wait()
    lax.fori_loop(0, row_count // BIG, adagrad, 0)
    store_table = pltpu.make_async_copy(table_out, table_hbm, sems.at[1])
    store_table.start()

    def publish(k, carry):
        rows = pl.ds(pl.multiple_of(k * BIG, BIG), BIG)
        delta = table_out[rows, :].astype(f32) - item_ref[rows, :].astype(f32)
        turned = lax.dot_general(
            eye_mark, jnp.abs(delta).astype(bf16), (((1,), (1,)), ((), ())),
            preferred_element_type=f32,
        )
        top = jnp.max(turned.reshape(LANES // 32, 32, BIG), axis=1)
        top = jnp.concatenate([jnp.maximum(top, SCALE_FLOOR), jnp.zeros((4, BIG), f32)], axis=0)
        scale = lax.dot_general(
            top.astype(bf16), spread, (((0,), (0,)), ((), ())), preferred_element_type=f32
        )
        payload = (delta / scale).astype(bf16)
        change_out[rows, :] = payload.astype(f32) * scale
        return carry

    lax.fori_loop(0, row_count // BIG, publish, 0)
    store_table.wait()


def stage_kernel(serving_hbm, *refs):
    out_ref, sem = refs[-2:]
    load = pltpu.make_async_copy(serving_hbm.at[pl.ds(0, out_ref.shape[0]), :], out_ref, sem)
    load.start()
    load.wait()


def apply_kernel(me_ref, change_ref, upper_ref, lower_ref, around_ref, serving_out, live_out):
    f32 = jnp.float32
    half = upper_ref.shape[0]
    turned = lax.rem(me_ref[0], 4) == 3
    lower = jnp.where(turned, around_ref[...].astype(f32), lower_ref[...].astype(f32))
    for start, old in ((0, upper_ref[...].astype(f32)), (half, lower)):
        serving = (old + change_ref[start : start + half, :]).astype(jnp.bfloat16)
        serving_out[start : start + half, :] = serving
        live_out[start : start + half, :] = serving.astype(f32)


def unroll_of(width):
    for unroll in (64, 32, 16):
        if width % unroll == 0:
            return unroll
    return width


def gather_kernel(moves, pitch, me_ref, ids_ref, live_ref, *outs):
    width = outs[0].shape[0]
    unroll = unroll_of(width)
    for move, out_ref in zip(moves, outs):
        start = lax.bitwise_xor(me_ref[0], move) * pitch

        def some(k, carry):
            at = start + k * unroll
            rows = [live_ref[pl.ds(ids_ref[at + u], 1), :] for u in range(unroll)]
            out_ref[pl.ds(pl.multiple_of(k * unroll, unroll), unroll), :] = jnp.concatenate(
                rows, axis=0
            ).astype(jnp.bfloat16)
            return carry

        lax.fori_loop(0, width // unroll, some, 0)


def gather_all_kernel(pitch, ids_ref, live_ref, out_ref):
    blocks, width, _ = out_ref.shape

    def block(b, carry):
        rows = [live_ref[pl.ds(ids_ref[b * pitch + u], 1), :] for u in range(width)]
        out_ref[b] = jnp.concatenate(rows, axis=0).astype(jnp.bfloat16)
        return carry

    lax.fori_loop(0, blocks, block, 0)


def hold_kernel(live_ref, *refs):
    refs[-1][...] = live_ref[...].astype(jnp.bfloat16)


def deliver_kernel(from_ref, out_hbm, sem):
    store = pltpu.make_async_copy(from_ref, out_hbm, sem)
    store.start()
    store.wait()


def token_kernel(token_ref, *refs):
    refs[-1][...] = token_ref[...]


def tower_kernel(
    moves, shape, token_ref, me_ref, slots_ref, cross_hbm, cross_bias_ref, tower_hbm,
    tower_bias_ref, score_ref, *refs,
):
    f32, bf16 = jnp.float32, jnp.bfloat16
    feats, requests = shape
    pieces = refs[:-9]
    out_ref, cross_ref, tower_ref, got_ref = refs[-9:-5]
    wide_ref, plane_a, plane_b, crossed_ref, sems = refs[-5:]
    planes = (plane_a, plane_b)
    me = me_ref[0]
    loads = []
    for k, piece in enumerate(pieces):
        start, width = 0, piece.shape[0]
        if moves is not None:
            start = pl.multiple_of(lax.bitwise_xor(me, moves[k]) * width, width)
        loads.append(
            pltpu.make_async_copy(piece, got_ref.at[pl.ds(start, width), :], sems.at[2 + k])
        )
    load_cross = pltpu.make_async_copy(cross_hbm, cross_ref, sems.at[0])
    load_tower = pltpu.make_async_copy(tower_hbm, tower_ref, sems.at[1])
    for load in loads:
        load.start()
    load_cross.start()
    load_tower.start()
    for load in loads:
        load.wait()
    wide_ref[...] = got_ref[...].astype(f32)
    chunk = 256
    batch = 64

    def collect(c):
        plane = planes[c % 2]
        for f in range(feats):
            for r in range(0, chunk, batch):
                at = f * requests + c * chunk + r
                rows = [wide_ref[pl.ds(slots_ref[at + u], 1), :] for u in range(batch)]
                for u in range(batch):
                    plane[f * chunk + r + u : f * chunk + r + u + 1, :] = rows[u]
                yield

    for _ in collect(0):
        pass
    load_cross.wait()
    layers = cross_ref.shape[0]
    for c in range(requests // chunk):
        plane = planes[c % 2]
        base = jnp.concatenate([plane[f * chunk : (f + 1) * chunk, :] for f in range(feats)], axis=1)
        coming = list(range(feats * chunk // batch)) if (c + 1) * chunk < requests else []
        batches = collect(c + 1) if coming else iter(())
        old = base.astype(bf16)
        for layer in range(layers):
            projected = jnp.dot(old, cross_ref[layer], preferred_element_type=f32)
            for _ in coming[layer::layers]:
                next(batches)
            projected = projected + cross_bias_ref[layer : layer + 1, :].astype(f32)
            old = (base * projected + old.astype(f32)).astype(bf16)
        crossed_ref[c * chunk : (c + 1) * chunk, :] = old
    load_tower.wait()
    hidden = tower_ref.shape[1]
    chunk = 1024
    total = jnp.zeros((requests, LANES), f32)
    for start in range(0, hidden, chunk):
        cols = slice(start, start + chunk)
        raw = jnp.dot(crossed_ref[...], tower_ref[:, cols], preferred_element_type=f32)
        raw = jnp.maximum(raw + tower_bias_ref[:, cols].astype(f32), 0.0)
        raw = raw * score_ref[:, cols].astype(f32)
        for q in range(chunk // LANES):
            total = total + raw[:, q * LANES : (q + 1) * LANES]
    eye = lax.broadcasted_iota(jnp.int32, (LANES, LANES), 0) == lax.broadcasted_iota(
        jnp.int32, (LANES, LANES), 1
    )
    for k in range(requests // LANES):
        column = jnp.sum(total[k * LANES : (k + 1) * LANES, :], axis=1, keepdims=True)
        out_ref[k : k + 1, :] = jnp.sum(jnp.where(eye, column, 0.0), axis=0, keepdims=True)


def body(
    item_table, row_accum, serving_table, grad_rows, grad_ids, grad_counts, request_ids,
    request_slots, cross_weight, cross_bias, tower_weight, tower_bias, score_weight,
):
    f32, bf16 = jnp.float32, jnp.bfloat16
    shards = lax.axis_size("shard")
    row_count, emb = item_table.shape
    cap, capr = grad_ids.shape[1], request_ids.shape[1]
    requests, feats = request_slots.shape
    req_rows = ceil_to(capr, LANES) // LANES
    meta_rows = ceil_to(2 + 2 * req_rows, 16)
    vmem = pl.BlockSpec(memory_space=pltpu.VMEM)
    smem = pl.BlockSpec(memory_space=pltpu.SMEM)
    hbm = pl.BlockSpec(memory_space=pltpu.HBM)

    def call(kernel, name, limit, **kwargs):
        params = pltpu.CompilerParams(vmem_limit_bytes=limit * MIB)
        return pl.pallas_call(kernel, name=name, compiler_params=params, **kwargs)

    me = lax.axis_index("shard").astype(jnp.int32).reshape(1)

    packed, aside = call(
        functools.partial(pack_kernel, cap, req_rows), "pack", 56,
        out_shape=(
            jax.ShapeDtypeStruct((shards, cap + meta_rows, emb), bf16),
            jax.ShapeDtypeStruct((row_count // 2, emb), bf16),
        ),
        in_specs=[hbm] * 4 + [smem],
        out_specs=(vmem, vmem),
        scratch_shapes=[
            pltpu.VMEM((shards, cap), jnp.int32),
            pltpu.VMEM((shards, capr), jnp.int32),
            pltpu.VMEM((shards, meta_rows, LANES), f32),
            pltpu.SemaphoreType.DMA((4,)),
        ],
    )(grad_rows, grad_ids, request_ids, serving_table, grad_counts)
    recv = lax.all_to_all(packed, "shard", split_axis=0, concat_axis=0, tiled=True)
    behind = [(i, (i - 1) % shards) for i in range(shards)]
    ahead = [(i, (i + 1) % shards) for i in range(shards)]
    slots = request_slots.T.reshape(-1)
    tower_bias, score_weight = tower_bias.reshape(1, -1), score_weight.reshape(1, -1)
    half = row_count // 2
    if shards == 16:
        straight = [(i, i - 1) for i in range(shards) if i % 4]
        lower = lax.ppermute(aside, "shard", straight + [(i, i + 3) for i in range(0, shards, 4)])
        upper = call(
            stage_kernel, "stage", 8,
            out_shape=jax.ShapeDtypeStruct((half, emb), bf16),
            in_specs=[hbm] * 5,
            out_specs=vmem,
            scratch_shapes=[pltpu.SemaphoreType.DMA],
            cost_estimate=work(1.0),
        )(serving_table, lower, slots, tower_bias, score_weight)
        upper = lax.ppermute(upper, "shard", behind)
        around = lax.ppermute(lower, "shard", [(3, 15), (7, 3), (11, 7), (15, 11)])
        serving_parts = (upper, lower, around)
    else:
        serving_here = lax.ppermute(serving_table, "shard", behind)
        serving_parts = (serving_here[:half], serving_here[half:], serving_here[half:])

    joined = recv
    if cap < LANES:
        groups = shards * cap // LANES
        marks = recv[:, cap : cap + 2, :cap].reshape(groups, LANES // cap, 2, cap)
        marks = marks.transpose(0, 2, 1, 3).reshape(groups, 2, LANES)
        marks = jnp.pad(marks, ((0, 0), (0, 14), (0, 0)))
        joined = jnp.concatenate([recv[:, :cap, :].reshape(groups, LANES, emb), marks], axis=1)

    new_table, new_accum, change, req = call(
        functools.partial(update_kernel, LANES, cap + 2, req_rows), "update", 32,
        out_shape=(
            jax.ShapeDtypeStruct((row_count, emb), bf16),
            jax.ShapeDtypeStruct((row_count // LANES, LANES), f32),
            jax.ShapeDtypeStruct((row_count, emb), f32),
            jax.ShapeDtypeStruct((shards, req_rows, LANES), jnp.int32),
        ),
        in_specs=[vmem, vmem, vmem, hbm],
        out_specs=(hbm, vmem, vmem, vmem),
        scratch_shapes=[
            pltpu.VMEM((shards * cap, 2 * LANES), bf16),
            pltpu.VMEM((row_count, LANES), f32),
            pltpu.VMEM((row_count, LANES), bf16),
            pltpu.VMEM((row_count, LANES), bf16),
            pltpu.SemaphoreType.DMA((2,)),
        ],
    )(joined, recv, row_accum.reshape(-1, LANES), item_table)
    serving_next, live = call(
        apply_kernel, "apply", 8,
        out_shape=(
            jax.ShapeDtypeStruct((row_count, emb), bf16),
            jax.ShapeDtypeStruct((row_count, emb), f32),
        ),
        in_specs=[smem] + [vmem] * 4,
        out_specs=(vmem, vmem),
    )(me, change, *serving_parts)
    req = req.reshape(-1)

    pitch = req_rows * LANES
    serving_next = live
    if shards == 16:
        moves, pieces = [], []
        for sends in SENDS:
            found = call(
                functools.partial(gather_kernel, sends, pitch), "gather", 4,
                out_shape=(jax.ShapeDtypeStruct((capr, emb), bf16),) * len(sends),
                in_specs=[smem, smem, vmem],
                out_specs=(vmem,) * len(sends),
                cost_estimate=work(0.6 * len(sends)),
            )(me, req, live)
            for move, rows in zip(sends, found):
                moves.append(move)
                if move == 0:
                    pieces.append(rows)
                    continue
                pieces.append(lax.ppermute(rows, "shard", [(i, i ^ move) for i in range(shards)]))
        token = jnp.zeros((8, LANES), f32)
        for takes in TAKES:
            token = call(
                token_kernel, "token", 4,
                out_shape=jax.ShapeDtypeStruct((8, LANES), f32),
                in_specs=[vmem] + [hbm] * len(takes),
                out_specs=vmem,
                cost_estimate=work(0.6 * len(takes) + 0.6),
            )(token, *[pieces[moves.index(move)] for move in takes])
    else:
        found = call(
            functools.partial(gather_all_kernel, pitch), "gather", 8,
            out_shape=jax.ShapeDtypeStruct((shards, capr, emb), bf16),
            in_specs=[smem, vmem],
            out_specs=vmem,
        )(req, live)
        moves, token = None, jnp.zeros((8, LANES), f32)
        got = lax.all_to_all(found, "shard", split_axis=0, concat_axis=0, tiled=True)
        pieces = [got.reshape(shards * capr, emb)]
    held = call(
        hold_kernel, "hold", 8,
        out_shape=jax.ShapeDtypeStruct((row_count, emb), bf16),
        in_specs=[vmem] + [hbm] * len(pieces),
        out_specs=vmem,
        cost_estimate=work(0.5),
    )(live, *pieces)
    sent = lax.ppermute(held, "shard", ahead)
    scores = call(
        functools.partial(tower_kernel, moves, (feats, requests)), "tower", 58,
        out_shape=jax.ShapeDtypeStruct((requests // LANES, LANES), f32),
        in_specs=[vmem] + [smem] * 2 + [hbm, vmem, hbm, vmem, vmem] + [hbm] * len(pieces),
        out_specs=vmem,
        scratch_shapes=[
            pltpu.VMEM(cross_weight.shape, bf16),
            pltpu.VMEM(tower_weight.shape, bf16),
            pltpu.VMEM((shards * capr, emb), bf16),
            pltpu.VMEM((shards * capr, emb), f32),
            pltpu.VMEM((feats * 256, emb), f32),
            pltpu.VMEM((feats * 256, emb), f32),
            pltpu.VMEM((requests, feats * emb), bf16),
            pltpu.SemaphoreType.DMA((2 + len(pieces),)),
        ],
    )(
        token, me, slots, cross_weight, cross_bias, tower_weight,
        tower_bias, score_weight, *pieces,
    )
    new_serving = call(
        deliver_kernel, "deliver", 8,
        out_shape=jax.ShapeDtypeStruct((row_count, emb), bf16),
        in_specs=[vmem],
        out_specs=hbm,
        scratch_shapes=[pltpu.SemaphoreType.DMA],
    )(sent)
    return (new_table, new_accum.reshape(row_count), new_serving, scores.reshape(requests))


def solution(mesh):
    both = ("groups", "shard")
    in_specs = (
        P("shard", None), P("shard"), P("shard", None), P(both, None, None), P(both, None), P(both),
        P(both, None), P(both, None), P(), P(), P(), P(), P(),
    )
    out_specs = (P(both, None), P(both), P(both, None), P(both))
    return jax.shard_map(body, mesh=mesh, in_specs=in_specs, out_specs=out_specs, check_vma=False)
```

```python
import functools
import jax
import jax.numpy as jnp
from jax import lax
from jax.experimental import pallas as pl
from jax.experimental.pallas import tpu as pltpu
from jax.sharding import PartitionSpec as P

LEARN_RATE = 0.5
SCALE_FLOOR = 0.25
LANES = 128
DIGIT = 64
TILE = 256
BIG = 2048
MIB = 1024 * 1024


def ceil_to(value, unit):
    return -(-value // unit) * unit


SENDS = ((8,), (9, 1), (10, 2, 11), (3, 12, 4), (13, 5, 14), (6, 15, 7, 0))
TAKES = ((8, 9, 1), (10, 2, 11), (3, 12, 4), (13, 5, 14))


def work(micros):
    return pl.CostEstimate(flops=0, transcendentals=0, bytes_accessed=int(micros * 3.0e6))


def pack_kernel(
    cap, req_rows, rows_hbm, ids_hbm, req_hbm, serving_hbm, counts_ref, out_ref, aside_ref,
    ids_ref, req_ref, meta_ref, sems,
):
    f32 = jnp.float32
    half = aside_ref.shape[0]
    loads = [
        pltpu.make_async_copy(ids_hbm, ids_ref, sems.at[0]),
        pltpu.make_async_copy(req_hbm, req_ref, sems.at[1]),
        pltpu.make_async_copy(rows_hbm, out_ref.at[:, :cap, :], sems.at[2]),
        pltpu.make_async_copy(serving_hbm.at[pl.ds(half, half), :], aside_ref, sems.at[3]),
    ]
    for load in loads:
        load.start()
    meta_ref[...] = jnp.zeros_like(meta_ref)
    slot = lax.broadcasted_iota(jnp.int32, ids_ref.shape, 1)
    block = lax.broadcasted_iota(jnp.int32, ids_ref.shape, 0)
    count = jnp.zeros(ids_ref.shape, jnp.int32)
    for b in range(ids_ref.shape[0]):
        count = jnp.where(block == b, counts_ref[b], count)
    loads[0].wait()
    ids = ids_ref[...]
    width = ids.shape[1]
    meta_ref[:, 0, :width] = jnp.where(slot < count, ids // TILE, TILE - 1).astype(f32)
    meta_ref[:, 1, :width] = (ids % TILE).astype(f32)
    loads[1].wait()
    for row in range(req_rows):
        start = row * LANES
        stop = min(start + LANES, req_ref.shape[1])
        part = req_ref[:, start:stop]
        meta_ref[:, 2 + row, : stop - start] = (part // DIGIT).astype(f32)
        meta_ref[:, 2 + req_rows + row, : stop - start] = (part % DIGIT).astype(f32)
    out_ref[:, cap:, :] = meta_ref[...].astype(jnp.bfloat16)
    loads[2].wait()
    loads[3].wait()


def update_kernel(
    cap, req_at, req_rows, recv_ref, req_ref, accum_ref, item_hbm,
    table_hbm, accum_out, change_out, req_out, pair_ref, grad_ref, item_ref, table_out, sems,
):
    load_item = pltpu.make_async_copy(item_hbm, item_ref, sems.at[0])
    load_item.start()
    f32, bf16 = jnp.float32, jnp.bfloat16
    blocks = recv_ref.shape[0]
    row_count = item_hbm.shape[0]
    half_tiles = row_count // TILE // 2
    req_high = req_ref[:, req_at : req_at + req_rows, :].astype(f32)
    req_low = req_ref[:, req_at + req_rows : req_at + 2 * req_rows, :].astype(f32)
    req_out[...] = (req_high * DIGIT + req_low).astype(jnp.int32)
    eye = lax.broadcasted_iota(jnp.int32, (LANES, LANES), 0) == lax.broadcasted_iota(
        jnp.int32, (LANES, LANES), 1
    )
    eye_mark = jnp.where(eye, 1.0, 0.0).astype(bf16)
    ones = jnp.ones((LANES, LANES), bf16)
    keys = []
    for b in range(blocks):
        high = recv_ref[b, cap : cap + 1, :].astype(f32)
        low = recv_ref[b, cap + 1 : cap + 2, :].astype(f32)
        upper = high >= half_tiles
        keys.append((jnp.where(upper, high - half_tiles, high), low))
        spots = jnp.where(eye, jnp.where(upper, 1.0, 0.0), 0.0).astype(bf16)
        side = jnp.dot(spots, ones, preferred_element_type=f32)
        rows = recv_ref[b, :cap, :].astype(f32)
        pair_ref[b * cap : (b + 1) * cap, :LANES] = jnp.where(side > 0.5, 0.0, rows).astype(bf16)
        pair_ref[b * cap : (b + 1) * cap, LANES:] = jnp.where(side > 0.5, rows, 0.0).astype(bf16)
    row_in_tile = lax.broadcasted_iota(jnp.int32, (TILE, LANES), 0).astype(jnp.int16)
    mark, blank = jnp.ones((), bf16), jnp.zeros((), bf16)
    lines = lax.broadcasted_iota(jnp.int32, (8, LANES), 0)
    spread = jnp.where(lines == lax.broadcasted_iota(jnp.int32, (8, LANES), 1) // 32, 1.0, 0.0)
    spread = spread.astype(bf16)
    part = lax.broadcasted_iota(jnp.int32, (4 * LANES, LANES), 0)
    weigh = jnp.where(part < 2 * LANES, 1.0 / LANES, 1.0).astype(bf16)

    def scatter(t, carry):
        here = t.astype(f32)
        marks = []
        for high, low in keys:
            key = jnp.where(high == here, low, -1.0).astype(jnp.int16)
            marks.append(jnp.where(row_in_tile == jnp.broadcast_to(key, (TILE, LANES)), mark, blank))
        grad = jnp.dot(jnp.concatenate(marks, axis=1), pair_ref[...], preferred_element_type=f32)
        rows = pl.multiple_of(t * TILE, TILE)
        grad_ref[pl.ds(rows, TILE), :] = grad[:, :LANES]
        grad_ref[pl.ds(rows + row_count // 2, TILE), :] = grad[:, LANES:]
        return carry

    lax.fori_loop(0, half_tiles, scatter, 0, unroll=2)

    def adagrad(k, carry):
        rows = pl.ds(pl.multiple_of(k * BIG, BIG), BIG)
        grad = grad_ref[rows, :]
        square = grad * grad
        coarse = square.astype(bf16)
        rest = (square - coarse.astype(f32)).astype(bf16)
        lines = [accum_ref[pl.ds(k * (BIG // LANES) + q, 1), :] for q in range(BIG // LANES)]
        upper = [line.astype(bf16).astype(f32) for line in lines]
        olds = [
            jnp.concatenate([jnp.where(eye, line, 0.0) for line in part], axis=0).astype(bf16)
            for part in (upper, [line - high for line, high in zip(lines, upper)])
        ]
        accum = jnp.dot(
            jnp.concatenate([coarse, rest, *olds], axis=1), weigh, preferred_element_type=f32
        )
        for q in range(BIG // LANES):
            mine = jnp.where(eye, accum[q * LANES : (q + 1) * LANES], 0.0)
            accum_out[pl.ds(k * (BIG // LANES) + q, 1), :] = jnp.sum(mine, axis=0, keepdims=True)
        item = item_ref[rows, :].astype(f32)
        table_out[rows, :] = (item - LEARN_RATE * grad * lax.rsqrt(accum)).astype(bf16)
        return carry

    load_item.wait()
    lax.fori_loop(0, row_count // BIG, adagrad, 0)
    store_table = pltpu.make_async_copy(table_out, table_hbm, sems.at[1])
    store_table.start()

    def publish(k, carry):
        rows = pl.ds(pl.multiple_of(k * BIG, BIG), BIG)
        delta = table_out[rows, :].astype(f32) - item_ref[rows, :].astype(f32)
        turned = lax.dot_general(
            eye_mark, jnp.abs(delta).astype(bf16), (((1,), (1,)), ((), ())),
            preferred_element_type=f32,
        )
        top = jnp.max(turned.reshape(LANES // 32, 32, BIG), axis=1)
        top = jnp.concatenate([jnp.maximum(top, SCALE_FLOOR), jnp.zeros((4, BIG), f32)], axis=0)
        scale = lax.dot_general(
            top.astype(bf16), spread, (((0,), (0,)), ((), ())), preferred_element_type=f32
        )
        payload = (delta / scale).astype(bf16)
        change_out[rows, :] = payload.astype(f32) * scale
        return carry

    lax.fori_loop(0, row_count // BIG, publish, 0)
    store_table.wait()


def stage_kernel(serving_hbm, *refs):
    out_ref, sem = refs[-2:]
    load = pltpu.make_async_copy(serving_hbm.at[pl.ds(0, out_ref.shape[0]), :], out_ref, sem)
    load.start()
    load.wait()


def apply_kernel(me_ref, change_ref, upper_ref, lower_ref, around_ref, live_out):
    f32 = jnp.float32
    half = upper_ref.shape[0]
    turned = lax.rem(me_ref[0], 4) == 3
    lower = jnp.where(turned, around_ref[...].astype(f32), lower_ref[...].astype(f32))
    for start, old in ((0, upper_ref[...].astype(f32)), (half, lower)):
        serving = (old + change_ref[start : start + half, :]).astype(jnp.bfloat16)
        live_out[start : start + half, :] = serving.astype(f32)


def unroll_of(width):
    for unroll in (64, 32, 16):
        if width % unroll == 0:
            return unroll
    return width


def gather_kernel(moves, pitch, me_ref, ids_ref, live_ref, *outs):
    width = outs[0].shape[0]
    unroll = unroll_of(width)
    for move, out_ref in zip(moves, outs):
        start = lax.bitwise_xor(me_ref[0], move) * pitch

        def some(k, carry):
            at = start + k * unroll
            rows = [live_ref[pl.ds(ids_ref[at + u], 1), :] for u in range(unroll)]
            out_ref[pl.ds(pl.multiple_of(k * unroll, unroll), unroll), :] = jnp.concatenate(
                rows, axis=0
            ).astype(jnp.bfloat16)
            return carry

        lax.fori_loop(0, width // unroll, some, 0)


def gather_all_kernel(pitch, ids_ref, live_ref, out_ref):
    blocks, width, _ = out_ref.shape

    def block(b, carry):
        rows = [live_ref[pl.ds(ids_ref[b * pitch + u], 1), :] for u in range(width)]
        out_ref[b] = jnp.concatenate(rows, axis=0).astype(jnp.bfloat16)
        return carry

    lax.fori_loop(0, blocks, block, 0)


def hold_kernel(live_ref, *refs):
    refs[-1][...] = live_ref[...].astype(jnp.bfloat16)


def deliver_kernel(from_ref, out_hbm, sem):
    store = pltpu.make_async_copy(from_ref, out_hbm, sem)
    store.start()
    store.wait()


def token_kernel(token_ref, *refs):
    refs[-1][...] = token_ref[...]


def tower_kernel(
    moves, shape, token_ref, me_ref, slots_ref, cross_hbm, cross_bias_ref, tower_hbm,
    tower_bias_ref, score_ref, *refs,
):
    f32, bf16 = jnp.float32, jnp.bfloat16
    feats, requests = shape
    pieces = refs[:-9]
    out_ref, cross_ref, tower_ref, got_ref = refs[-9:-5]
    wide_ref, plane_a, plane_b, crossed_ref, sems = refs[-5:]
    planes = (plane_a, plane_b)
    me = me_ref[0]
    loads = []
    for k, piece in enumerate(pieces):
        start, width = 0, piece.shape[0]
        if moves is not None:
            start = pl.multiple_of(lax.bitwise_xor(me, moves[k]) * width, width)
        loads.append(
            pltpu.make_async_copy(piece, got_ref.at[pl.ds(start, width), :], sems.at[2 + k])
        )
    load_cross = pltpu.make_async_copy(cross_hbm, cross_ref, sems.at[0])
    load_tower = pltpu.make_async_copy(tower_hbm, tower_ref, sems.at[1])
    for load in loads:
        load.start()
    load_cross.start()
    load_tower.start()
    for load in loads:
        load.wait()
    wide_ref[...] = got_ref[...].astype(f32)
    chunk = 256
    batch = 64

    def collect(c):
        plane = planes[c % 2]
        for f in range(feats):
            for r in range(0, chunk, batch):
                at = f * requests + c * chunk + r
                rows = [wide_ref[pl.ds(slots_ref[at + u], 1), :] for u in range(batch)]
                for u in range(batch):
                    plane[f * chunk + r + u : f * chunk + r + u + 1, :] = rows[u]
                yield

    for _ in collect(0):
        pass
    load_cross.wait()
    layers = cross_ref.shape[0]
    for c in range(requests // chunk):
        plane = planes[c % 2]
        base = jnp.concatenate([plane[f * chunk : (f + 1) * chunk, :] for f in range(feats)], axis=1)
        coming = list(range(feats * chunk // batch)) if (c + 1) * chunk < requests else []
        batches = collect(c + 1) if coming else iter(())
        old = base.astype(bf16)
        for layer in range(layers):
            projected = jnp.dot(old, cross_ref[layer], preferred_element_type=f32)
            for _ in coming[layer::layers]:
                next(batches)
            projected = projected + cross_bias_ref[layer : layer + 1, :].astype(f32)
            old = (base * projected + old.astype(f32)).astype(bf16)
        crossed_ref[c * chunk : (c + 1) * chunk, :] = old
    load_tower.wait()
    hidden = tower_ref.shape[1]
    chunk = 1024
    total = jnp.zeros((requests, LANES), f32)
    for start in range(0, hidden, chunk):
        cols = slice(start, start + chunk)
        raw = jnp.dot(crossed_ref[...], tower_ref[:, cols], preferred_element_type=f32)
        raw = jnp.maximum(raw + tower_bias_ref[:, cols].astype(f32), 0.0)
        raw = raw * score_ref[:, cols].astype(f32)
        for q in range(chunk // LANES):
            total = total + raw[:, q * LANES : (q + 1) * LANES]
    eye = lax.broadcasted_iota(jnp.int32, (LANES, LANES), 0) == lax.broadcasted_iota(
        jnp.int32, (LANES, LANES), 1
    )
    for k in range(requests // LANES):
        column = jnp.sum(total[k * LANES : (k + 1) * LANES, :], axis=1, keepdims=True)
        out_ref[k : k + 1, :] = jnp.sum(jnp.where(eye, column, 0.0), axis=0, keepdims=True)


def body(
    item_table, row_accum, serving_table, grad_rows, grad_ids, grad_counts, request_ids,
    request_slots, cross_weight, cross_bias, tower_weight, tower_bias, score_weight,
):
    f32, bf16 = jnp.float32, jnp.bfloat16
    shards = lax.axis_size("shard")
    row_count, emb = item_table.shape
    cap, capr = grad_ids.shape[1], request_ids.shape[1]
    requests, feats = request_slots.shape
    req_rows = ceil_to(capr, LANES) // LANES
    meta_rows = ceil_to(2 + 2 * req_rows, 16)
    vmem = pl.BlockSpec(memory_space=pltpu.VMEM)
    smem = pl.BlockSpec(memory_space=pltpu.SMEM)
    hbm = pl.BlockSpec(memory_space=pltpu.HBM)

    def call(kernel, name, limit, **kwargs):
        params = pltpu.CompilerParams(vmem_limit_bytes=limit * MIB)
        return pl.pallas_call(kernel, name=name, compiler_params=params, **kwargs)

    me = lax.axis_index("shard").astype(jnp.int32).reshape(1)

    packed, aside = call(
        functools.partial(pack_kernel, cap, req_rows), "pack", 56,
        out_shape=(
            jax.ShapeDtypeStruct((shards, cap + meta_rows, emb), bf16),
            jax.ShapeDtypeStruct((row_count // 2, emb), bf16),
        ),
        in_specs=[hbm] * 4 + [smem],
        out_specs=(vmem, vmem),
        scratch_shapes=[
            pltpu.VMEM((shards, cap), jnp.int32),
            pltpu.VMEM((shards, capr), jnp.int32),
            pltpu.VMEM((shards, meta_rows, LANES), f32),
            pltpu.SemaphoreType.DMA((4,)),
        ],
    )(grad_rows, grad_ids, request_ids, serving_table, grad_counts)
    recv = lax.all_to_all(packed, "shard", split_axis=0, concat_axis=0, tiled=True)
    behind = [(i, (i - 1) % shards) for i in range(shards)]
    ahead = [(i, (i + 1) % shards) for i in range(shards)]
    slots = request_slots.T.reshape(-1)
    tower_bias, score_weight = tower_bias.reshape(1, -1), score_weight.reshape(1, -1)
    half = row_count // 2
    if shards == 16:
        straight = [(i, i - 1) for i in range(shards) if i % 4]
        lower = lax.ppermute(aside, "shard", straight + [(i, i + 3) for i in range(0, shards, 4)])
        upper = call(
            stage_kernel, "stage", 8,
            out_shape=jax.ShapeDtypeStruct((half, emb), bf16),
            in_specs=[hbm] * 5,
            out_specs=vmem,
            scratch_shapes=[pltpu.SemaphoreType.DMA],
            cost_estimate=work(1.0),
        )(serving_table, lower, slots, tower_bias, score_weight)
        upper = lax.ppermute(upper, "shard", behind)
        around = lax.ppermute(lower, "shard", [(3, 15), (7, 3), (11, 7), (15, 11)])
        serving_parts = (upper, lower, around)
    else:
        serving_here = lax.ppermute(serving_table, "shard", behind)
        serving_parts = (serving_here[:half], serving_here[half:], serving_here[half:])

    joined = recv
    if cap < LANES:
        groups = shards * cap // LANES
        marks = recv[:, cap : cap + 2, :cap].reshape(groups, LANES // cap, 2, cap)
        marks = marks.transpose(0, 2, 1, 3).reshape(groups, 2, LANES)
        marks = jnp.pad(marks, ((0, 0), (0, 14), (0, 0)))
        joined = jnp.concatenate([recv[:, :cap, :].reshape(groups, LANES, emb), marks], axis=1)

    new_table, new_accum, change, req = call(
        functools.partial(update_kernel, LANES, cap + 2, req_rows), "update", 32,
        out_shape=(
            jax.ShapeDtypeStruct((row_count, emb), bf16),
            jax.ShapeDtypeStruct((row_count // LANES, LANES), f32),
            jax.ShapeDtypeStruct((row_count, emb), f32),
            jax.ShapeDtypeStruct((shards, req_rows, LANES), jnp.int32),
        ),
        in_specs=[vmem, vmem, vmem, hbm],
        out_specs=(hbm, vmem, vmem, vmem),
        scratch_shapes=[
            pltpu.VMEM((shards * cap, 2 * LANES), bf16),
            pltpu.VMEM((row_count, LANES), f32),
            pltpu.VMEM((row_count, LANES), bf16),
            pltpu.VMEM((row_count, LANES), bf16),
            pltpu.SemaphoreType.DMA((2,)),
        ],
    )(joined, recv, row_accum.reshape(-1, LANES), item_table)
    live = call(
        apply_kernel, "apply", 8,
        out_shape=jax.ShapeDtypeStruct((row_count, emb), f32),
        in_specs=[smem] + [vmem] * 4,
        out_specs=vmem,
    )(me, change, *serving_parts)
    req = req.reshape(-1)

    pitch = req_rows * LANES
    if shards == 16:
        moves, pieces = [], []
        for sends in SENDS:
            found = call(
                functools.partial(gather_kernel, sends, pitch), "gather", 4,
                out_shape=(jax.ShapeDtypeStruct((capr, emb), bf16),) * len(sends),
                in_specs=[smem, smem, vmem],
                out_specs=(vmem,) * len(sends),
                cost_estimate=work(0.6 * len(sends)),
            )(me, req, live)
            for move, rows in zip(sends, found):
                moves.append(move)
                if move == 0:
                    pieces.append(rows)
                    continue
                pieces.append(lax.ppermute(rows, "shard", [(i, i ^ move) for i in range(shards)]))
        token = jnp.zeros((8, LANES), f32)
        for takes in TAKES:
            token = call(
                token_kernel, "token", 4,
                out_shape=jax.ShapeDtypeStruct((8, LANES), f32),
                in_specs=[vmem] + [hbm] * len(takes),
                out_specs=vmem,
                cost_estimate=work(0.6 * len(takes) + 0.6),
            )(token, *[pieces[moves.index(move)] for move in takes])
    else:
        found = call(
            functools.partial(gather_all_kernel, pitch), "gather", 8,
            out_shape=jax.ShapeDtypeStruct((shards, capr, emb), bf16),
            in_specs=[smem, vmem],
            out_specs=vmem,
        )(req, live)
        moves, token = None, jnp.zeros((8, LANES), f32)
        got = lax.all_to_all(found, "shard", split_axis=0, concat_axis=0, tiled=True)
        pieces = [got.reshape(shards * capr, emb)]
    held = call(
        hold_kernel, "hold", 8,
        out_shape=jax.ShapeDtypeStruct((row_count, emb), bf16),
        in_specs=[vmem] + [hbm] * len(pieces),
        out_specs=vmem,
        cost_estimate=work(0.5),
    )(live, *pieces)
    sent = lax.ppermute(held, "shard", ahead)
    scores = call(
        functools.partial(tower_kernel, moves, (feats, requests)), "tower", 58,
        out_shape=jax.ShapeDtypeStruct((requests // LANES, LANES), f32),
        in_specs=[vmem] + [smem] * 2 + [hbm, vmem, hbm, vmem, vmem] + [hbm] * len(pieces),
        out_specs=vmem,
        scratch_shapes=[
            pltpu.VMEM(cross_weight.shape, bf16),
            pltpu.VMEM(tower_weight.shape, bf16),
            pltpu.VMEM((shards * capr, emb), bf16),
            pltpu.VMEM((shards * capr, emb), f32),
            pltpu.VMEM((feats * 256, emb), f32),
            pltpu.VMEM((feats * 256, emb), f32),
            pltpu.VMEM((requests, feats * emb), bf16),
            pltpu.SemaphoreType.DMA((2 + len(pieces),)),
        ],
    )(
        token, me, slots, cross_weight, cross_bias, tower_weight,
        tower_bias, score_weight, *pieces,
    )
    new_serving = call(
        deliver_kernel, "deliver", 8,
        out_shape=jax.ShapeDtypeStruct((row_count, emb), bf16),
        in_specs=[vmem],
        out_specs=hbm,
        scratch_shapes=[pltpu.SemaphoreType.DMA],
    )(sent)
    return (new_table, new_accum.reshape(row_count), new_serving, scores.reshape(requests))


def solution(mesh):
    both = ("groups", "shard")
    in_specs = (
        P("shard", None), P("shard"), P("shard", None), P(both, None, None), P(both, None), P(both),
        P(both, None), P(both, None), P(), P(), P(), P(), P(),
    )
    out_specs = (P(both, None), P(both), P(both, None), P(both))
    return jax.shard_map(body, mesh=mesh, in_specs=in_specs, out_specs=out_specs, check_vma=False)
```
